256 devices in a mesh: sub: 256 (over y, z, x, core).
Axes of the slice: x: 4, y: 4, z: 8, core: 2. Of those that a mesh axis runs over, the one named last changes fastest.
Arguments:
- jumps: float32 [256, 1536, 128], P('sub'), may hold values from -6 to 6
- schur: bfloat16 [256, 1536, 1536], P('sub'), as said below
- coupling: float32 [256, 24, 1536], P('sub'), may hold values from -0.4375 to 0.4375
- coarse_inverse: float32 [768, 768], replicated, as said below
- scaling: float32 [256, 1536], P('sub'), as said below
- glued: int32 [256, 6], P('sub'), may hold values from 0 to 1, as said below
- matching: int32 [256, 6, 256], P('sub'), may hold values from 0 to 255, as said below
- corners: int32 [256, 24], P('sub'), may hold values from 0 to 767, all different within a row
Outputs:
- multipliers: float32 [256, 1536, 128], P('sub')
- residual: float32 [256, 1536, 128], P('sub')
The draws below stay inside these ranges and needn't reach their ends.
Inputs may be any that keep to these rules, and one draw needn't show every extreme that they name: Subdomain s sits at x = s % 4, y = (s // 4) % 4, z = s // 16; 1 where a face is glued to its neighbour in the grid, 0 where it is not or where the grid has no neighbour; both sides of a face agree. `matching`: each row is a permutation of 0 to 255; the row of face 2d + 1 of the upper neighbour is the inverse of the row of face 2d. `corners`: each row names 24 different coarse dofs, and every coarse dof is named by some row. `schur`: each block is symmetric positive definite. `coarse_inverse`: symmetric positive definite. `scaling`: positive, and equal at the two dofs of every glued match.
All inputs are finite; a program needn't handle non-finite values.
Results may differ from the reference program's by a relative error of at most 0.013.
Values sent between devices are 32-bit elements; how exact they have to be, the bound alone decides.
No kernel may reach another device: no remote copies, remote signals or barrier semaphores. Data moves between devices by JAX's collectives and lax.ppermute only.
A program may use at most 128 MiB of HBM per device.

```python
import math
import jax
import jax.numpy as jnp
from jax import lax

FS = 16
FD = 256
I = 1536
LOADS = 128
CL = 24
ITERS = 5
GX = 4
GY = 4
NSUB = 256
GZ = 16
NC = 768


rough_terms = 4


def face_geometry(jitter):
    dof_ids = jnp.arange(I, dtype=jnp.int32)
    face = dof_ids // FD
    within = dof_ids % FD
    first = (within % FS).astype(jnp.float32)
    second = (within // FS).astype(jnp.float32)
    along_u = (first + 0.5 + jitter[:, 0]) / FS
    along_w = (second + 0.5 + jitter[:, 1]) / FS
    side = (1 - face % 2).astype(jnp.float32)
    axis_id = face // 2
    coord_x = jnp.where(axis_id == 0, side, along_u)
    coord_y = jnp.where(axis_id == 1, side, jnp.where(axis_id == 0, along_u, along_w))
    coord_z = jnp.where(axis_id == 2, side, along_w)
    return (coord_x, coord_y, coord_z)


def draw_schur(key, part):
    key = jax.random.fold_in(key, 11)
    jitter_key, diagonal_key, phase_key = jax.random.split(key, 3)
    reach = 0.15
    diagonal = jnp.exp(jax.random.uniform(diagonal_key, (NSUB, I), jnp.float32, math.log(0.3), math.log(1.2)))
    jitter = jax.random.uniform(jitter_key, (NSUB, I, 2), jnp.float32, -0.35, 0.35)
    phases = jax.random.uniform(phase_key, (NSUB, I, rough_terms), jnp.float32, -math.pi, math.pi)
    strength = 40.0 / (I * reach / (reach + 0.8))

    def single(triple):
        jitter_one, diagonal_one, phase_one = triple
        coord_x, coord_y, coord_z = face_geometry(jitter_one)
        distance = jnp.sqrt((coord_x[:, None] - coord_x[None, :]) ** 2 + (coord_y[:, None] - coord_y[None, :]) ** 2 + (coord_z[:, None] - coord_z[None, :]) ** 2)
        kernel = strength * reach / (reach + distance)
        cosines = jnp.cos(phase_one)
        sines = jnp.sin(phase_one)
        texture = jnp.full((I, I), 0.5, jnp.float32)
        for term in range(rough_terms):
            texture = texture + 0.5 / rough_terms * (cosines[:, term][:, None] * cosines[:, term][None, :] + sines[:, term][:, None] * sines[:, term][None, :])
        block = kernel * texture + jnp.diag(diagonal_one)
        return block.astype(jnp.bfloat16)
    return lax.map(single, (jitter, diagonal, phases))


def draw_coarse_inverse(key, part):
    key = jax.random.fold_in(key, 13)
    jitter_key, diagonal_key = jax.random.split(key)
    jitter = jax.random.uniform(jitter_key, (NC,), jnp.float32, -0.3, 0.3)
    places = 0.1 * (jnp.arange(NC).astype(jnp.float32) + jitter)
    strength = 0.15
    diagonal = jnp.exp(jax.random.uniform(diagonal_key, (NC,), jnp.float32, math.log(0.2), math.log(1.0)))
    return strength * jnp.exp(-jnp.abs(places[:, None] - places[None, :]) / 0.3) + jnp.diag(diagonal)


def pair_tables(key):
    glue_key, perm_key = jax.random.split(key)
    sub_ids = jnp.arange(NSUB, dtype=jnp.int32)
    coord_x = sub_ids % GX
    coord_y = sub_ids // GX % GY
    coord_z = sub_ids // (GX * GY)
    exists = jnp.stack([coord_x < GX - 1, coord_y < GY - 1, coord_z < GZ - 1], 1)
    glue_up = (jax.random.randint(glue_key, (NSUB, 3), 0, 20) < 17) & exists
    perm_keys = jax.random.split(perm_key, NSUB * 3)
    perm_up = jax.vmap(lambda single_key: jax.random.permutation(single_key, FD))(perm_keys).reshape(NSUB, 3, FD).astype(jnp.int32)
    perm_down = jnp.argsort(perm_up, axis=2).astype(jnp.int32)
    glue_cols = []
    perm_cols = []
    for direction, stride in enumerate((1, GX, GX * GY)):
        lower_ids = sub_ids - stride
        valid = lower_ids >= 0
        safe_ids = jnp.clip(lower_ids, 0, NSUB - 1)
        glue_cols.append(glue_up[:, direction])
        glue_cols.append(valid & glue_up[safe_ids, direction])
        perm_cols.append(perm_up[:, direction])
        perm_cols.append(perm_down[safe_ids, direction])
    glued = jnp.stack(glue_cols, 1).astype(jnp.int32)
    matching = jnp.stack(perm_cols, 1).astype(jnp.int32)
    return (glued, matching)


def draw_glued(key, part):
    glued, matching = pair_tables(key)
    return glued


def draw_matching(key, part):
    glued, matching = pair_tables(key)
    return matching


def draw_scaling(key, part):
    glued, matching = pair_tables(key)
    key = jax.random.fold_in(key, 17)
    upper_weights = jnp.exp(jax.random.uniform(key, (NSUB, 3, FD), jnp.float32, math.log(0.5), math.log(2.0)))
    sub_ids = jnp.arange(NSUB, dtype=jnp.int32)
    columns = []
    for direction, stride in enumerate((1, GX, GX * GY)):
        safe_ids = jnp.clip(sub_ids - stride, 0, NSUB - 1)
        columns.append(upper_weights[:, direction])
        columns.append(jnp.take_along_axis(upper_weights[safe_ids, direction], matching[:, 2 * direction + 1], axis=1))
    return jnp.stack(columns, 1).reshape(NSUB, I)


def level_of(stream_key, extent, pieces, low, high):
    factor_of = 1.0
    for position, blocks in pieces:
        steps = jax.random.uniform(jax.random.fold_in(jax.random.fold_in(stream_key, 6), position), (blocks,), jnp.float32, low / len(pieces), high / len(pieces))
        factor_of = factor_of * jnp.repeat(jnp.exp(steps), extent[position] // blocks).reshape((-1,) + (1,) * (len(extent) - 1 - position))
    return factor_of


def distinct(rng, rows, count, top, lift):
    ranking = jax.random.permutation(jax.random.fold_in(rng, 1), count)
    favour = ranking
    for power in range(3):
        favour = favour * favour // count
    favour = favour * lift // count
    tickets = jax.random.randint(jax.random.fold_in(rng, 2), (rows, count), 0, 4096) + favour
    sure = jax.random.permutation(jax.random.fold_in(rng, 3), rows)[jnp.arange(count) % rows]
    tickets = jnp.where(jnp.arange(rows)[:, None] == sure[None, :], 1 << 14, tickets)
    priority = tickets * count + jnp.arange(count)
    return lax.top_k(priority.astype(jnp.int32), top)[1].astype(jnp.int32)


def centred(key, shape, spread, bound, pieces=(), kind=jnp.bfloat16):
    values = jax.random.normal(key, shape, jnp.float32) * spread
    if len(pieces) > 0:
        values = level_of(key, shape, pieces, -0.22, 0.18) * values
    return jnp.clip(values, min=-bound, max=bound).astype(kind)


def setup_inputs(seed: int = 0) -> dict:
    splits = jax.random.split(jax.random.key(seed), 9)
    jumps = centred(splits[0], (NSUB, I, LOADS), 1.0, 6.0, ((0, 256),), jnp.float32)
    schur = draw_schur(jax.random.fold_in(splits[8], 71), 0)
    coupling = centred(splits[2], (NSUB, CL, I), (I // 8) ** -0.5, 0.4375, ((0, 256),), jnp.float32)
    coarse_inverse = draw_coarse_inverse(jax.random.fold_in(splits[8], 71), 0)
    scaling = draw_scaling(jax.random.fold_in(splits[8], 71), 0)
    glued = draw_glued(jax.random.fold_in(splits[8], 71), 0)
    matching = draw_matching(jax.random.fold_in(splits[8], 71), 0)
    corners = distinct(splits[7], NSUB, NC, CL, 0)
    return {"jumps": jumps, "schur": schur, "coupling": coupling, "coarse_inverse": coarse_inverse, "scaling": scaling, "glued": glued, "matching": matching, "corners": corners}


def assemble(values, glued, matching):
    count_sub = values.shape[0]
    blocks = values.reshape(count_sub, 6, FD, LOADS)
    sub_ids = jnp.arange(count_sub, dtype=jnp.int32)
    strides = (1, GX, GX * GY)
    partner_rows = []
    for face in range(6):
        stride = strides[face // 2]
        if face % 2 == 0:
            other = sub_ids + stride
            source = face + 1
        else:
            other = sub_ids - stride
            source = face - 1
        other = jnp.clip(other, 0, count_sub - 1).astype(jnp.int32)
        rows = blocks[other, source]
        rows = jnp.take_along_axis(rows, matching[:, face, :, None].astype(jnp.int32), axis=1)
        partner_rows.append(rows)
    partner = jnp.stack(partner_rows, 1).reshape(count_sub, 6 * FD, LOADS)
    glue_mask = jnp.repeat(glued.astype(jnp.float32), FD, axis=1)[:, :, None]
    return glue_mask * (values + partner)


def reference(jumps, schur, coupling, coarse_inverse, scaling, glued, matching, corners):
    face_sign = jnp.repeat(jnp.array([1.0, -1.0, 1.0, -1.0, 1.0, -1.0], jnp.float32), FD)[None, :, None]
    highest = lax.Precision.HIGHEST

    def operate(values):
        signed = face_sign * values
        signed_b = signed.astype(jnp.bfloat16)
        local_part = lax.map(lambda pair: jnp.dot(pair[0], pair[1], preferred_element_type=jnp.float32), (schur, signed_b))
        corner_terms = jnp.einsum("sci,sil->scl", coupling, signed, precision=highest)
        coarse = jnp.zeros((NC, LOADS), jnp.float32).at[corners.reshape(-1)].add(corner_terms.reshape(-1, LOADS))
        coarse_solution = jnp.dot(coarse_inverse, coarse, precision=highest)
        nearby = coarse_solution[corners]
        local_image = local_part + jnp.einsum("sci,scl->sil", coupling, nearby, precision=highest)
        return assemble(face_sign * local_image, glued, matching)

    gap = assemble(face_sign * jumps, glued, matching)
    weights = scaling[:, :, None]
    multipliers = jnp.zeros_like(gap)
    residual = gap
    precond = weights * residual
    energy_now = 0.5 * jnp.sum(residual * precond, axis=(0, 1))
    direction = precond
    for iteration in range(ITERS):
        product = operate(direction)
        step_size = energy_now / (0.5 * jnp.sum(direction * product, axis=(0, 1)))
        multipliers = multipliers + step_size * direction
        residual = residual - step_size * product
        precond = weights * residual
        energy_next = 0.5 * jnp.sum(residual * precond, axis=(0, 1))
        direction = precond + (energy_next / energy_now) * direction
        energy_now = energy_next
    return multipliers, residual
```

```python
import jax
import jax.numpy as jnp
import numpy as np
from jax import lax
from jax.sharding import PartitionSpec as P

ITERS = 5
STRIDES = (1, 4, 16)
GRID = (4, 4, 16)
NSUB = 256
PLACES = np.arange(NSUB).reshape(4, 8, 8)
PLANES = PLACES.transpose(1, 0, 2).reshape(8, 32).tolist()
LINES = PLACES.transpose(0, 2, 1).reshape(32, 8).tolist()
PLANE = 32
LINE = 8
DOTS = 8


def route(direction, sign):
    stride, extent = STRIDES[direction], GRID[direction]
    pairs = []
    for i in range(NSUB):
        place = i // stride % extent
        if 0 <= place + sign < extent:
            pairs.append((i, i + sign * stride))
    return pairs


UP = [route(d, 1) for d in range(3)]
DOWN = [route(d, -1) for d in range(3)]


def swap_faces(blocks):
    received = []
    for d in range(3):
        received.append(lax.ppermute(blocks[2 * d + 1], "sub", DOWN[d]))
        received.append(lax.ppermute(blocks[2 * d], "sub", UP[d]))
    return received


def dot(a, b, dims=(((1,), (0,)), ((), ())), precision=lax.Precision.HIGH):
    return lax.dot_general(a, b, dims, precision=precision, preferred_element_type=jnp.float32)


def total_of(terms, dots, selector):
    spread = dot(selector, terms, precision=lax.Precision.HIGHEST).reshape(PLANE, -1, terms.shape[1])
    rows = spread.shape[1]
    packed = jnp.concatenate([spread, jnp.broadcast_to(dots[None], (PLANE,) + dots.shape)], 1)
    packed = lax.all_to_all(packed, "sub", 0, 0, axis_index_groups=PLANES)
    own = jnp.sum(packed, 0)
    own = lax.all_to_all(
        jnp.broadcast_to(own[None], (LINE,) + own.shape), "sub", 0, 0, axis_index_groups=LINES
    )
    own = jnp.sum(own, 0)
    whole = lax.all_to_all(
        jnp.broadcast_to(own[None, :rows], (PLANE, rows, own.shape[1])),
        "sub",
        0,
        0,
        axis_index_groups=PLANES,
    )
    return whole.reshape(PLANE * rows, -1), own[rows:]


def shards(jumps, schur, coupling, coarse_inverse, scaling, glued, matching, corners):
    highest = lax.Precision.HIGHEST
    faces, fd = matching.shape[1:]
    loads = jumps.shape[2]
    dofs = faces * fd
    coarse_count = coarse_inverse.shape[0]
    corner_ids = corners[0]
    corner_count = corner_ids.shape[0]
    mask = jnp.repeat(glued[0].astype(jnp.float32), fd)[:, None]
    links = matching[0]

    place = lax.broadcasted_iota(jnp.int32, (fd, fd), 0)
    orders = jnp.stack([(place == links[2 * d + 1][None, :]) for d in range(3)])
    orders_b = orders.astype(jnp.bfloat16)
    orders_f = orders.astype(jnp.float32)

    def reorder_rows(values, back=False):
        blocks = values.reshape(3, 2, fd, values.shape[1])
        dims = (((1 if back else 2,), (1,)), ((0,), (0,)))
        if values.dtype == jnp.bfloat16:
            odd = dot(orders_b, blocks[:, 1], dims, None).astype(jnp.bfloat16)
        else:
            odd = dot(orders_f, blocks[:, 1], dims, highest)
        return jnp.stack([blocks[:, 0], odd], 1)

    def flip(blocks):
        return jnp.stack([blocks[:, 0], -blocks[:, 1]], 1).reshape(dofs, -1)

    jump = flip(reorder_rows(jumps[0]))
    couple_t = flip(reorder_rows(coupling[0].T))
    couple = couple_t.T
    weights = reorder_rows(jnp.broadcast_to(scaling[0][:, None], (dofs, loads))).reshape(dofs, loads)

    sent = []
    id_rows = jnp.zeros((8, loads), jnp.float32).at[0, :corner_count].set(corner_ids.astype(jnp.float32))
    for f in range(faces):
        part = couple[:, f * fd : (f + 1) * fd]
        sent.append(
            jnp.concatenate(
                [jump[f * fd : (f + 1) * fd], part[:, :loads], part[:, loads:], id_rows], 0
            )
        )
    got = swap_faces(sent)

    half = flip(reorder_rows(schur[0]))
    schur_block = flip(reorder_rows(half.T))

    gap = mask * (jump + jnp.concatenate([g[:fd] for g in got], 0))
    lift_rows = [couple * mask[:, 0][None, :]]
    near_ids = [corner_ids]
    for f in range(faces):
        part = jnp.concatenate(
            [got[f][fd : fd + corner_count], got[f][fd + corner_count : fd + 2 * corner_count]], 1
        )
        part = part * mask[f * fd, 0]
        lift_rows.append(jnp.pad(part, ((0, 0), (f * fd, dofs - (f + 1) * fd))))
        near_ids.append(got[f][fd + 2 * corner_count, :corner_count].astype(jnp.int32))
    lift = jnp.concatenate(lift_rows, 0).T
    near_ids = jnp.concatenate(near_ids)
    near_inverse = coarse_inverse[near_ids]
    selector = (
        lax.broadcasted_iota(jnp.int32, (coarse_count, corner_count), 0) == corner_ids[None, :]
    ).astype(jnp.float32)

    multipliers = jnp.zeros_like(gap)
    residual = gap
    direction = image = None
    energy = curvature = None
    for iteration in range(ITERS):
        precond = weights * residual
        rounded = precond.astype(jnp.bfloat16)
        terms = dot(couple, precond)
        local = dot(schur_block, rounded, precision=None)
        received = swap_faces([local[f * fd : (f + 1) * fd] for f in range(faces)])
        dots = [0.5 * jnp.sum(residual * precond, 0), jnp.sum(precond * local, 0)]
        if iteration:
            dots.append(0.5 * jnp.sum(precond * image, 0))
        dots += [jnp.zeros_like(dots[0])] * (DOTS - len(dots))
        coarse, sums = total_of(terms, jnp.stack(dots), selector)
        near = dot(near_inverse, coarse)
        product = mask * (local + jnp.concatenate(received, 0)) + dot(lift, near)
        energy_next = sums[0]
        bend = sums[1] + jnp.sum(coarse * dot(coarse_inverse, coarse), 0)
        if iteration:
            ratio = energy_next / energy
            curvature = bend + ratio * (2.0 * sums[2] + ratio * curvature)
            direction = precond + ratio * direction
            image = product + ratio * image
        else:
            curvature = bend
            direction = precond
            image = product
        energy = energy_next
        step = energy / curvature
        multipliers = multipliers + step * direction
        residual = residual - step * image

    multipliers = reorder_rows(multipliers, True).reshape(1, dofs, loads)
    residual = reorder_rows(residual, True).reshape(1, dofs, loads)
    return (multipliers, residual)


def solution(mesh):
    return jax.shard_map(
        shards,
        mesh=mesh,
        in_specs=(
            P("sub", None, None),
            P("sub", None, None),
            P("sub", None, None),
            P(),
            P("sub", None),
            P("sub", None),
            P("sub", None, None),
            P("sub", None),
        ),
        out_specs=(P("sub", None, None), P("sub", None, None)),
        check_vma=False,
    )
```

```python
import functools

import jax
import jax.numpy as jnp
import numpy as np
from jax import lax
from jax.experimental import pallas as pl
from jax.experimental.pallas import tpu as pltpu
from jax.sharding import PartitionSpec as P

ITERS = 5
STRIDES = (1, 4, 16)
GRID = (4, 4, 16)
NSUB = 256
FACES = 6
FD = 256
DOFS = FACES * FD
LOADS = 128
CORNERS = 24
COARSE = 768
NEAR = 256
DOTS = 8
PACKED = FD + 2 * CORNERS + 8
PLACES = np.arange(NSUB).reshape(4, 8, 8)
PLANES = PLACES.transpose(1, 0, 2).reshape(8, 32).tolist()
LINES = PLACES.transpose(0, 2, 1).reshape(32, 8).tolist()
PLANE = 32
LINE = 8
ROWS = COARSE // PLANE
f32 = jnp.float32
bf16 = jnp.bfloat16


def route(direction, sign):
    stride, extent = STRIDES[direction], GRID[direction]
    pairs = []
    for i in range(NSUB):
        place = i // stride % extent
        if 0 <= place + sign < extent:
            pairs.append((i, i + sign * stride))
    return pairs


UP = [route(d, 1) for d in range(3)]
DOWN = [route(d, -1) for d in range(3)]


def swap_faces(blocks):
    received = []
    for d in range(3):
        received.append(lax.ppermute(blocks[2 * d + 1], "sub", DOWN[d]))
        received.append(lax.ppermute(blocks[2 * d], "sub", UP[d]))
    return received


def call(kernel, outs, inputs, smem=(), scratch=(), flops=0):
    shapes = [jax.ShapeDtypeStruct(s, t) for s, t in outs]
    size = sum(int(np.prod(s)) * jnp.dtype(t).itemsize for s, t in outs)
    size += sum(x.size * x.dtype.itemsize for x in inputs)
    return pl.pallas_call(
        kernel,
        out_shape=shapes,
        in_specs=[
            pl.BlockSpec(memory_space=pltpu.SMEM if i in smem else pltpu.VMEM)
            for i in range(len(inputs))
        ],
        out_specs=[pl.BlockSpec(memory_space=pltpu.VMEM)] * len(outs),
        scratch_shapes=list(scratch),
        compiler_params=pltpu.CompilerParams(vmem_limit_bytes=40 * 2**20),
        cost_estimate=pl.CostEstimate(flops=flops, bytes_accessed=size, transcendentals=0),
    )(*inputs)


def mm(a, b):
    return lax.dot_general(a, b, (((1,), (0,)), ((), ())), preferred_element_type=f32)


def mm_t(a, b):
    return lax.dot_general(a, b, (((1,), (1,)), ((), ())), preferred_element_type=f32)


def split(values):
    high = values.astype(bf16)
    return high, (values - high.astype(f32)).astype(bf16)


def split3(values):
    high = values.astype(bf16)
    rest = values - high.astype(f32)
    middle = rest.astype(bf16)
    return high, middle, (rest - middle.astype(f32)).astype(bf16)


def face(f):
    return slice(f * FD, (f + 1) * FD)


def order_of(links_ref, f):
    place = lax.broadcasted_iota(jnp.int32, (FD, FD), 0)
    return jnp.where(place == links_ref[f : f + 1, :], 1.0, 0.0).astype(bf16)


def reorder(order, values):
    high, middle, low = split3(values)
    both = mm(order, jnp.concatenate([high, middle], 1))
    return both[:, :LOADS] + both[:, LOADS:] + mm(order, low)


def pack_kernel(jumps, coupling, links, ids, couple, *packs):
    for f in range(FACES):
        part = coupling[:, face(f)]
        jump = jumps[face(f), :]
        if f % 2:
            order = order_of(links, f)
            jump = -reorder(order, jump)
            high, middle, low = split3(part)
            part = -(mm_t(high, order) + mm_t(middle, order) + mm_t(low, order))
        couple[:, face(f)] = part
        packs[f][:FD, :] = jump
        packs[f][FD : FD + CORNERS, :] = part[:, :LOADS]
        packs[f][FD + CORNERS : FD + 2 * CORNERS, :] = part[:, LOADS:]
        packs[f][FD + 2 * CORNERS :, :] = ids[...]


def arrange_kernel(schur, links, weights, schur_out, weights_out, half):
    for f in range(FACES):
        if f % 2:
            order = order_of(links, f)
            half[face(f), :] = (-mm(order, schur[face(f), :])).astype(bf16)
            weights_out[face(f), :] = reorder(order, weights[face(f), :])
        else:
            half[face(f), :] = schur[face(f), :]
            weights_out[face(f), :] = weights[face(f), :]
    for f in range(FACES):
        if f % 2:
            order = order_of(links, f)
            schur_out[:, face(f)] = (-mm_t(half[:, face(f)], order)).astype(bf16)
        else:
            schur_out[:, face(f)] = half[:, face(f)]


def lift_kernel(*refs):
    glued, couple = refs[:2]
    packs = refs[2 : 2 + FACES]
    high, low, rows = refs[2 + FACES :]
    for f in range(FACES):
        mask = glued[0, f].astype(f32)
        rows[...] = jnp.zeros_like(rows)
        rows[:CORNERS, :] = couple[:, face(f)] * mask
        start = CORNERS * (f + 1)
        rows[start : start + CORNERS, :LOADS] = packs[f][FD : FD + CORNERS, :] * mask
        rows[start : start + CORNERS, LOADS:] = packs[f][FD + CORNERS : FD + 2 * CORNERS, :] * mask
        both = split(rows[...].T)
        high[face(f), :] = both[0]
        low[face(f), :] = both[1]


def open_precond(weights, couple, ids, residual, precond, rounded, spread, state):
    terms = jnp.zeros((2 * CORNERS, 2 * LOADS), f32)
    energy = jnp.zeros((1, LOADS), f32)
    couple_high, couple_low = split(couple[...])
    stacked = jnp.concatenate([couple_high.astype(f32), couple_low.astype(f32)], 0).astype(bf16)
    for f in range(FACES):
        now = weights[face(f), :] * residual[face(f), :]
        precond[face(f), :] = now
        energy += jnp.sum(now * residual[face(f), :], 0, keepdims=True)
        high, low = split(now)
        rounded[face(f), :] = high
        terms += mm(stacked[:, face(f)], jnp.concatenate([high, low], 1))
    terms = terms[:, :LOADS] + terms[:, LOADS:]
    terms = terms[:CORNERS] + terms[CORNERS:]
    spread[...] = jnp.zeros_like(spread)
    for j in range(CORNERS):
        spread[pl.ds(ids[0, j], 1), :] = terms[j : j + 1]
    state[0:1, :] = 0.5 * energy


def begin_kernel(*refs):
    glued, ids, couple, weights = refs[:4]
    sent = refs[4 : 4 + FACES]
    got = refs[4 + FACES : 4 + 2 * FACES]
    residual, precond, rounded, spread, state = refs[4 + 2 * FACES :]
    state[...] = jnp.zeros_like(state)
    for f in range(FACES):
        mask = glued[0, f].astype(f32)
        residual[face(f), :] = mask * (sent[f][:FD, :] + got[f][:FD, :])
    open_precond(weights, couple, ids, residual, precond, rounded, spread, state)


def local_kernel(schur, rounded, precond, state, *refs):
    faces, dots = refs[:FACES], refs[FACES]
    bend = jnp.zeros((1, LOADS), f32)
    for f in range(FACES):
        now = mm(schur[face(f), :], rounded[...])
        faces[f][...] = now
        bend += jnp.sum(now * precond[face(f), :], 0, keepdims=True)
    dots[...] = state[...]
    dots[1:2, :] = bend


def fold_plane_kernel(parts, dots, out):
    total = jnp.sum(parts[...], 0)
    for i in range(LINE):
        out[i, :ROWS, :] = total
        out[i, ROWS:, :] = dots[...]


def fold_line_kernel(parts, out):
    total = jnp.sum(parts[...], 0)
    for i in range(PLANE):
        out[i] = total


def advance_kernel(first, last, *refs):
    glued, ids, near_ids, whole, inverse_high, inverse_low, lift_high, lift_low = refs[:8]
    refs = refs[8:]
    local, got, refs = refs[:FACES], refs[FACES : 2 * FACES], refs[2 * FACES :]
    weights, precond, residual, history = refs[:4]
    refs = refs[4:]
    if not first:
        multipliers, direction, image = refs[:3]
        refs = refs[3:]
    if last:
        links, multipliers_out, residual_out, solved, near = refs
    else:
        couple, multipliers_out, residual_out, direction_out, image_out = refs[:5]
        history_out, precond_out, rounded, spread, state, solved, near = refs[5:]

    coarse = whole[:, :ROWS, :].reshape(COARSE, LOADS)
    sums = jnp.sum(whole[:, ROWS:, :], 0)
    coarse_high, coarse_low = split(coarse)
    both = mm(inverse_high[...], jnp.concatenate([coarse_high, coarse_low], 1))
    solution_rows = both[:, :LOADS] + both[:, LOADS:] + mm(inverse_low[...], coarse_high)
    solved[...] = solution_rows
    near[...] = jnp.zeros_like(near)
    for j in range(CORNERS * (FACES + 1)):
        near[pl.ds(j, 1), :] = solved[pl.ds(near_ids[0, j], 1), :]
    near_high, near_low = split(near[...])
    near_both = jnp.concatenate([near_high, near_low], 1)

    energy = sums[0:1]
    curvature = sums[1:2] + jnp.sum(coarse * solution_rows, 0, keepdims=True)
    if not first:
        ratio = energy / history[0:1, :]
        curvature = curvature + ratio * (2.0 * sums[2:3] + ratio * history[1:2, :])
    step = energy / curvature
    if not last:
        history_out[0:1, :] = energy
        history_out[1:2, :] = curvature
        state[...] = jnp.zeros_like(state)
    cross = jnp.zeros((1, LOADS), f32)
    for f in range(FACES):
        mask = glued[0, f].astype(f32)
        lift = mm(lift_high[face(f), :], near_both)
        lift = lift[:, :LOADS] + lift[:, LOADS:] + mm(lift_low[face(f), :], near_high)
        now = mask * (local[f][...] + got[f][...]) + lift
        way = precond[face(f), :]
        if not first:
            now = now + ratio * image[face(f), :]
            way = way + ratio * direction[face(f), :]
        move = step * way
        if not first:
            move = multipliers[face(f), :] + move
        rest = residual[face(f), :] - step * now
        if last:
            if f % 2:
                place = lax.broadcasted_iota(jnp.int32, (FD, FD), 0)
                order = jnp.where(place == links[f : f + 1, :], 1.0, 0.0).T.astype(bf16)
                move = reorder(order, move)
                rest = reorder(order, rest)
            multipliers_out[face(f), :] = move
            residual_out[face(f), :] = rest
        else:
            multipliers_out[face(f), :] = move
            residual_out[face(f), :] = rest
            direction_out[face(f), :] = way
            image_out[face(f), :] = now
            cross += jnp.sum(weights[face(f), :] * rest * now, 0, keepdims=True)
    if not last:
        open_precond(weights, couple, ids, residual_out, precond_out, rounded, spread, state)
        state[2:3, :] = 0.5 * cross


def shards(jumps, schur, coupling, coarse_inverse, scaling, glued, matching, corners):
    links = matching[0]
    field = ((DOFS, LOADS), f32)
    small = ((DOTS, LOADS), f32)
    open_outs = [field, ((DOFS, LOADS), bf16), ((COARSE, LOADS), f32), small]

    ids_row = jnp.pad(corners.astype(f32), ((0, 7), (0, LOADS - CORNERS)))
    couple, *sent = call(
        pack_kernel,
        [((CORNERS, DOFS), f32)] + [((PACKED, LOADS), f32)] * FACES,
        [jumps[0], coupling[0], links, ids_row],
    )
    got = swap_faces(sent)
    schur_block, weights = call(
        arrange_kernel,
        [((DOFS, DOFS), bf16), field],
        [schur[0], links, jnp.broadcast_to(scaling[0][:, None], (DOFS, LOADS))],
        scratch=[pltpu.VMEM((DOFS, DOFS), bf16)],
        flops=4 * DOFS * DOFS * FD,
    )
    residual, precond, rounded, spread, state = call(
        begin_kernel, [field] + open_outs, [glued, corners, couple, weights, *sent, *got], smem=(0, 1)
    )
    lift_high, lift_low = call(
        lift_kernel,
        [((DOFS, NEAR), bf16)] * 2,
        [glued, couple, *got],
        smem=(0,),
        scratch=[pltpu.VMEM((NEAR, FD), f32)],
    )
    near_ids = jnp.concatenate(
        [corners] + [g[FD + 2 * CORNERS :][:1, :CORNERS].astype(jnp.int32) for g in got], 1
    )
    kept = lax.reduce_precision(coarse_inverse, 8, 7)
    inverse_high, inverse_low = kept.astype(bf16), (coarse_inverse - kept).astype(bf16)

    multipliers = direction = image = history = None
    for iteration in range(ITERS):
        first, last = iteration == 0, iteration + 1 == ITERS
        parts = lax.all_to_all(
            spread.reshape(PLANE, ROWS, LOADS), "sub", 0, 0, axis_index_groups=PLANES
        )
        *local, dots = call(
            local_kernel,
            [((FD, LOADS), f32)] * FACES + [small],
            [schur_block, rounded, precond, state],
            flops=2 * DOFS * DOFS * LOADS,
        )
        received = swap_faces(local)
        (lines,) = call(fold_plane_kernel, [((LINE, ROWS + DOTS, LOADS), f32)], [parts, dots])
        lines = lax.all_to_all(lines, "sub", 0, 0, axis_index_groups=LINES)
        (whole,) = call(fold_line_kernel, [((PLANE, ROWS + DOTS, LOADS), f32)], [lines])
        whole = lax.all_to_all(whole, "sub", 0, 0, axis_index_groups=PLANES)
        inputs = [glued, corners, near_ids, whole, inverse_high, inverse_low, lift_high, lift_low]
        inputs += [*local, *received, weights, precond, residual]
        inputs += [state if first else history]
        if not first:
            inputs += [multipliers, direction, image]
        inputs += [links if last else couple]
        outs = [field, field]
        if not last:
            outs += [field, field, small] + open_outs
        results = call(
            functools.partial(advance_kernel, first, last),
            outs,
            inputs,
            smem=(0, 1, 2),
            scratch=[pltpu.VMEM((COARSE, LOADS), f32), pltpu.VMEM((NEAR, LOADS), f32)],
        )
        multipliers, residual = results[:2]
        if not last:
            direction, image, history, precond, rounded, spread, state = results[2:]
    return (multipliers[None], residual[None])


def solution(mesh):
    return jax.shard_map(
        shards,
        mesh=mesh,
        in_specs=(
            P("sub", None, None),
            P("sub", None, None),
            P("sub", None, None),
            P(),
            P("sub", None),
            P("sub", None),
            P("sub", None, None),
            P("sub", None),
        ),
        out_specs=(P("sub", None, None), P("sub", None, None)),
        check_vma=False,
    )
```

```python
import functools

import jax
import jax.numpy as jnp
import numpy as np
from jax import lax
from jax.experimental import pallas as pl
from jax.experimental.pallas import tpu as pltpu
from jax.sharding import PartitionSpec as P

ITERS = 5
STRIDES = (1, 4, 16)
GRID = (4, 4, 16)
NSUB = 256
FACES = 6
FD = 256
DOFS = FACES * FD
LOADS = 128
CORNERS = 24
COARSE = 768
NEAR = 256
DOTS = 8
EARLY = (0, 1, 2)
LATE = (3, 4, 5)
PACKED = FD + 2 * CORNERS + 8
PLACES = np.arange(NSUB).reshape(4, 8, 8)
PLANES = PLACES.transpose(1, 0, 2).reshape(8, 32).tolist()
LINES = PLACES.transpose(0, 2, 1).reshape(32, 8).tolist()
PLANE = 32
LINE = 8
ROWS = COARSE // PLANE
f32 = jnp.float32
bf16 = jnp.bfloat16


def route(direction, sign):
    stride, extent = STRIDES[direction], GRID[direction]
    pairs = []
    for i in range(NSUB):
        place = i // stride % extent
        if 0 <= place + sign < extent:
            pairs.append((i, i + sign * stride))
    return pairs


UP = [route(d, 1) for d in range(3)]
DOWN = [route(d, -1) for d in range(3)]


def swap_face(blocks, f):
    return lax.ppermute(blocks[f ^ 1], "sub", UP[f // 2] if f % 2 else DOWN[f // 2])


def call(kernel, outs, inputs, smem=(), anywhere=(), alias={}, scratch=(), flops=0, grant=8):
    shapes = [jax.ShapeDtypeStruct(s, t) for s, t in outs]
    size = sum(int(np.prod(s)) * jnp.dtype(t).itemsize for s, t in outs)
    size += sum(x.size * x.dtype.itemsize for x in inputs)
    return pl.pallas_call(
        kernel,
        out_shape=shapes,
        in_specs=[
            pl.BlockSpec(
                memory_space=pltpu.SMEM if i in smem else pl.ANY if i in anywhere else pltpu.VMEM
            )
            for i in range(len(inputs))
        ],
        out_specs=[
            pl.BlockSpec(memory_space=pl.ANY if i in alias.values() else pltpu.VMEM)
            for i in range(len(outs))
        ],
        input_output_aliases=alias,
        scratch_shapes=list(scratch),
        compiler_params=pltpu.CompilerParams(vmem_limit_bytes=grant * 2**20),
        cost_estimate=pl.CostEstimate(flops=flops, bytes_accessed=size, transcendentals=0),
    )(*inputs)


def mm(a, b):
    return lax.dot_general(a, b, (((1,), (0,)), ((), ())), preferred_element_type=f32)


def mm_t(a, b):
    return lax.dot_general(a, b, (((1,), (1,)), ((), ())), preferred_element_type=f32)


def split(values):
    high = values.astype(bf16)
    return high, (values - high.astype(f32)).astype(bf16)


def split3(values):
    high = values.astype(bf16)
    rest = values - high.astype(f32)
    middle = rest.astype(bf16)
    return high, middle, (rest - middle.astype(f32)).astype(bf16)


def face(f):
    return slice(f * FD, (f + 1) * FD)


def order_of(links_ref, f):
    place = lax.broadcasted_iota(jnp.int32, (FD, FD), 0)
    return jnp.where(place == links_ref[f : f + 1, :], 1.0, 0.0).astype(bf16)


def reorder(order, values):
    high, middle, low = split3(values)
    both = mm(order, jnp.concatenate([high, middle], 1))
    return both[:, :LOADS] + both[:, LOADS:] + mm(order, low)


def pack_kernel(jumps, coupling, links, ids, couple, *packs):
    for f in range(FACES):
        part = coupling[:, face(f)]
        jump = jumps[face(f), :]
        if f % 2:
            order = order_of(links, f)
            jump = -reorder(order, jump)
            high, middle, low = split3(part)
            part = -(mm_t(high, order) + mm_t(middle, order) + mm_t(low, order))
        couple[:, face(f)] = part
        packs[f][:FD, :] = jump
        packs[f][FD : FD + CORNERS, :] = part[:, :LOADS]
        packs[f][FD + CORNERS : FD + 2 * CORNERS, :] = part[:, LOADS:]
        packs[f][FD + 2 * CORNERS :, :] = ids[...]


def arrange_kernel(schur, links, weights, schur_out, weights_out, half):
    for f in range(FACES):
        if f % 2:
            order = order_of(links, f)
            half[face(f), :] = (-mm(order, schur[face(f), :])).astype(bf16)
            weights_out[face(f), :] = reorder(order, weights[face(f), :])
        else:
            half[face(f), :] = schur[face(f), :]
            weights_out[face(f), :] = weights[face(f), :]
    for f in range(FACES):
        if f % 2:
            order = order_of(links, f)
            schur_out[:, face(f)] = (-mm_t(half[:, face(f)], order)).astype(bf16)
        else:
            schur_out[:, face(f)] = half[:, face(f)]


def lift_kernel(*refs):
    glued, couple = refs[:2]
    packs = refs[2 : 2 + FACES]
    high, low, rows = refs[2 + FACES :]
    for f in range(FACES):
        mask = glued[0, f].astype(f32)
        rows[...] = jnp.zeros_like(rows)
        rows[:CORNERS, :] = couple[:, face(f)] * mask
        start = CORNERS * (f + 1)
        rows[start : start + CORNERS, :LOADS] = packs[f][FD : FD + CORNERS, :] * mask
        rows[start : start + CORNERS, LOADS:] = packs[f][FD + CORNERS : FD + 2 * CORNERS, :] * mask
        both = split(rows[...].T)
        high[face(f), :] = both[0]
        low[face(f), :] = both[1]


def open_precond(weights, couple, ids, residual, precond, rounded, spread, state):
    terms = jnp.zeros((2 * CORNERS, 2 * LOADS), f32)
    energy = jnp.zeros((1, LOADS), f32)
    couple_high, couple_low = split(couple[...])
    stacked = jnp.concatenate([couple_high.astype(f32), couple_low.astype(f32)], 0).astype(bf16)
    for f in range(FACES):
        now = weights[face(f), :] * residual[face(f), :]
        precond[face(f), :] = now
        energy += jnp.sum(now * residual[face(f), :], 0, keepdims=True)
        high, low = split(now)
        rounded[face(f), :] = high
        terms += mm(stacked[:, face(f)], jnp.concatenate([high, low], 1))
    terms = terms[:, :LOADS] + terms[:, LOADS:]
    terms = terms[:CORNERS] + terms[CORNERS:]
    spread[...] = jnp.zeros_like(spread)
    for j in range(CORNERS):
        spread[pl.ds(ids[0, j], 1), :] = terms[j : j + 1]
    state[0:1, :] = 0.5 * energy


def begin_kernel(*refs):
    glued, ids, couple, weights = refs[:4]
    sent = refs[4 : 4 + FACES]
    got = refs[4 + FACES : 4 + 2 * FACES]
    residual, precond, rounded, spread, state = refs[4 + 2 * FACES :]
    state[...] = jnp.zeros_like(state)
    for f in range(FACES):
        mask = glued[0, f].astype(f32)
        residual[face(f), :] = mask * (sent[f][:FD, :] + got[f][:FD, :])
    open_precond(weights, couple, ids, residual, precond, rounded, spread, state)


def local_kernel(schur, rounded, precond, state, *refs):
    faces, dots = refs[:FACES], refs[FACES]
    bend = jnp.zeros((1, LOADS), f32)
    for f in range(FACES):
        now = mm(schur[face(f), :], rounded[...])
        faces[f][...] = now
        bend += jnp.sum(now * precond[face(f), :], 0, keepdims=True)
    dots[...] = state[...]
    dots[1:2, :] = bend


def fold_plane_kernel(parts, dots, *refs):
    out = refs[-1]
    total = jnp.sum(parts[...], 0)
    for i in range(LINE):
        out[i, :ROWS, :] = total
        out[i, ROWS:, :] = dots[...]


def fold_line_kernel(parts, *refs):
    out = refs[len(refs) // 2]
    total = jnp.sum(parts[...], 0)
    for i in range(PLANE):
        out[i] = total


def advance_kernel(first, last, *refs):
    glued, ids, near_ids, whole, inverse_high, inverse_low, lift_high, lift_low = refs[:8]
    refs = refs[8:]
    local, got, refs = refs[:FACES], refs[FACES : 2 * FACES], refs[2 * FACES :]
    weights, precond, residual, history = refs[:4]
    refs = refs[4:]
    if not first:
        multipliers, direction, image = refs[:3]
        refs = refs[3:]
    if last:
        links, multipliers_out, residual_out, solved, near = refs
    else:
        couple, multipliers_out, residual_out, direction_out, image_out = refs[:5]
        history_out, precond_out, rounded, spread, state, solved, near = refs[5:]

    coarse = whole[:, :ROWS, :].reshape(COARSE, LOADS)
    sums = jnp.sum(whole[:, ROWS:, :], 0)
    coarse_high, coarse_low = split(coarse)
    both = mm(inverse_high[...], jnp.concatenate([coarse_high, coarse_low], 1))
    solution_rows = both[:, :LOADS] + both[:, LOADS:] + mm(inverse_low[...], coarse_high)
    solved[...] = solution_rows
    near[...] = jnp.zeros_like(near)
    for j in range(CORNERS * (FACES + 1)):
        near[pl.ds(j, 1), :] = solved[pl.ds(near_ids[0, j], 1), :]
    near_high, near_low = split(near[...])
    near_both = jnp.concatenate([near_high, near_low], 1)

    energy = sums[0:1]
    curvature = sums[1:2] + jnp.sum(coarse * solution_rows, 0, keepdims=True)
    if not first:
        ratio = energy / history[0:1, :]
        curvature = curvature + ratio * (2.0 * sums[2:3] + ratio * history[1:2, :])
    step = energy / curvature
    if not last:
        history_out[0:1, :] = energy
        history_out[1:2, :] = curvature
        state[...] = jnp.zeros_like(state)
    cross = jnp.zeros((1, LOADS), f32)
    for f in range(FACES):
        mask = glued[0, f].astype(f32)
        lift = mm(lift_high[face(f), :], near_both)
        lift = lift[:, :LOADS] + lift[:, LOADS:] + mm(lift_low[face(f), :], near_high)
        now = mask * (local[f][...] + got[f][...]) + lift
        way = precond[face(f), :]
        if not first:
            now = now + ratio * image[face(f), :]
            way = way + ratio * direction[face(f), :]
        move = step * way
        if not first:
            move = multipliers[face(f), :] + move
        rest = residual[face(f), :] - step * now
        if last:
            if f % 2:
                place = lax.broadcasted_iota(jnp.int32, (FD, FD), 0)
                order = jnp.where(place == links[f : f + 1, :], 1.0, 0.0).T.astype(bf16)
                move = reorder(order, move)
                rest = reorder(order, rest)
            multipliers_out[face(f), :] = move
            residual_out[face(f), :] = rest
        else:
            multipliers_out[face(f), :] = move
            residual_out[face(f), :] = rest
            direction_out[face(f), :] = way
            image_out[face(f), :] = now
            cross += jnp.sum(weights[face(f), :] * rest * now, 0, keepdims=True)
    if not last:
        open_precond(weights, couple, ids, residual_out, precond_out, rounded, spread, state)
        state[2:3, :] = 0.5 * cross


def shards(jumps, schur, coupling, coarse_inverse, scaling, glued, matching, corners):
    links = matching[0]
    field = ((DOFS, LOADS), f32)
    small = ((DOTS, LOADS), f32)
    open_outs = [field, ((DOFS, LOADS), bf16), ((COARSE, LOADS), f32), small]

    ids_row = jnp.pad(corners.astype(f32), ((0, 7), (0, LOADS - CORNERS)))
    couple, *sent = call(
        pack_kernel,
        [((CORNERS, DOFS), f32)] + [((PACKED, LOADS), f32)] * FACES,
        [jumps[0], coupling[0], links, ids_row],
    )
    got = [swap_face(sent, f) for f in range(FACES)]
    schur_block, weights = call(
        arrange_kernel,
        [((DOFS, DOFS), bf16), field],
        [schur[0], links, jnp.broadcast_to(scaling[0][:, None], (DOFS, LOADS))],
        scratch=[pltpu.VMEM((DOFS, DOFS), bf16)],
        flops=4 * DOFS * DOFS * FD,
        grant=16,
    )
    residual, precond, rounded, spread, state = call(
        begin_kernel, [field] + open_outs, [glued, corners, couple, weights, *sent, *got], smem=(0, 1)
    )
    lift_high, lift_low = call(
        lift_kernel,
        [((DOFS, NEAR), bf16)] * 2,
        [glued, couple, *got],
        smem=(0,),
        scratch=[pltpu.VMEM((NEAR, FD), f32)],
    )
    near_ids = jnp.concatenate(
        [corners] + [g[FD + 2 * CORNERS :][:1, :CORNERS].astype(jnp.int32) for g in got], 1
    )
    kept = lax.reduce_precision(coarse_inverse, 8, 7)
    inverse_high, inverse_low = kept.astype(bf16), (coarse_inverse - kept).astype(bf16)

    multipliers = direction = image = history = None
    for iteration in range(ITERS):
        first, last = iteration == 0, iteration + 1 == ITERS
        parts = lax.all_to_all(
            spread.reshape(PLANE, ROWS, LOADS), "sub", 0, 0, axis_index_groups=PLANES
        )
        *local, dots = call(
            local_kernel,
            [((FD, LOADS), f32)] * FACES + [small],
            [schur_block, rounded, precond, state],
            flops=2 * DOFS * DOFS * LOADS,
        )
        received = [None] * FACES
        for f in EARLY:
            received[f] = swap_face(local, f)
        early = [received[f] for f in EARLY]
        (lines,) = call(
            fold_plane_kernel,
            [((LINE, ROWS + DOTS, LOADS), f32)],
            [parts, dots, *early],
            anywhere=range(2, 2 + len(early)),
        )
        lines = lax.all_to_all(lines, "sub", 0, 0, axis_index_groups=LINES)
        held = [f ^ 1 for f in LATE]
        whole, *kept = call(
            fold_line_kernel,
            [((PLANE, ROWS + DOTS, LOADS), f32)] + [((FD, LOADS), f32)] * len(held),
            [lines, *[local[f] for f in held]],
            anywhere=range(1, 1 + len(held)),
            alias={1 + i: 1 + i for i in range(len(held))},
        )
        for f, block in zip(held, kept):
            local[f] = block
        whole = lax.all_to_all(whole, "sub", 0, 0, axis_index_groups=PLANES)
        for f in LATE:
            received[f] = swap_face(local, f)
        inputs = [glued, corners, near_ids, whole, inverse_high, inverse_low, lift_high, lift_low]
        inputs += [*local, *received, weights, precond, residual]
        inputs += [state if first else history]
        if not first:
            inputs += [multipliers, direction, image]
        inputs += [links if last else couple]
        outs = [field, field]
        if not last:
            outs += [field, field, small] + open_outs
        results = call(
            functools.partial(advance_kernel, first, last),
            outs,
            inputs,
            smem=(0, 1, 2),
            scratch=[pltpu.VMEM((COARSE, LOADS), f32), pltpu.VMEM((NEAR, LOADS), f32)],
        )
        multipliers, residual = results[:2]
        if not last:
            direction, image, history, precond, rounded, spread, state = results[2:]
    return (multipliers[None], residual[None])


def solution(mesh):
    return jax.shard_map(
        shards,
        mesh=mesh,
        in_specs=(
            P("sub", None, None),
            P("sub", None, None),
            P("sub", None, None),
            P(),
            P("sub", None),
            P("sub", None),
            P("sub", None, None),
            P("sub", None),
        ),
        out_specs=(P("sub", None, None), P("sub", None, None)),
        check_vma=False,
    )
```

```python
import functools

import jax
import jax.numpy as jnp
import numpy as np
from jax import lax
from jax.experimental import pallas as pl
from jax.experimental.pallas import tpu as pltpu
from jax.sharding import PartitionSpec as P

ITERS = 5
STRIDES = (1, 4, 16)
GRID = (4, 4, 16)
NSUB = 256
FACES = 6
FD = 256
DOFS = FACES * FD
LOADS = 128
CORNERS = 24
COARSE = 768
NEAR = 256
DOTS = 8
PACKED = FD + 2 * CORNERS + 8
PLACES = np.arange(NSUB).reshape(4, 8, 8)
PLANES = PLACES.transpose(1, 0, 2).reshape(8, 32).tolist()
LINES = PLACES.transpose(0, 2, 1).reshape(32, 8).tolist()
PLANE = 32
LINE = 8
ROWS = COARSE // PLANE
f32 = jnp.float32
bf16 = jnp.bfloat16


def route(direction, sign):
    stride, extent = STRIDES[direction], GRID[direction]
    pairs = []
    for i in range(NSUB):
        place = i // stride % extent
        if 0 <= place + sign < extent:
            pairs.append((i, i + sign * stride))
    return pairs


UP = [route(d, 1) for d in range(3)]
DOWN = [route(d, -1) for d in range(3)]


def swap_faces(blocks):
    received = []
    for d in range(3):
        received.append(lax.ppermute(blocks[2 * d + 1], "sub", DOWN[d]))
        received.append(lax.ppermute(blocks[2 * d], "sub", UP[d]))
    return received


def block_of(shape, kind):
    if kind == "smem":
        return pl.BlockSpec(memory_space=pltpu.SMEM)
    if kind == "rows":
        return pl.BlockSpec((FD, shape[1]), lambda f: (f, 0))
    if kind == "columns":
        return pl.BlockSpec((shape[0], FD), lambda f: (0, f))
    return pl.BlockSpec(shape, lambda f: (0,) * len(shape))


def call(kernel, steps, outs, inputs, scratch=(), flops=0):
    inputs = [x if isinstance(x, tuple) else (x, "whole") for x in inputs]
    outs = [x if len(x) == 3 else (*x, "whole") for x in outs]
    size = sum(int(np.prod(s)) * jnp.dtype(t).itemsize for s, t, _ in outs)
    size += sum(x.size * x.dtype.itemsize for x, _ in inputs)
    return pl.pallas_call(
        kernel,
        grid=(steps,),
        out_shape=[jax.ShapeDtypeStruct(s, t) for s, t, _ in outs],
        in_specs=[block_of(x.shape, kind) for x, kind in inputs],
        out_specs=[block_of(s, kind) for s, _, kind in outs],
        scratch_shapes=list(scratch),
        compiler_params=pltpu.CompilerParams(vmem_limit_bytes=56 * 2**20),
        cost_estimate=pl.CostEstimate(flops=flops, bytes_accessed=size, transcendentals=0),
    )(*[x for x, _ in inputs])


def mm(a, b):
    return lax.dot_general(a, b, (((1,), (0,)), ((), ())), preferred_element_type=f32)


def mm_t(a, b):
    return lax.dot_general(a, b, (((1,), (1,)), ((), ())), preferred_element_type=f32)


def split(values):
    high = values.astype(bf16)
    return high, (values - high.astype(f32)).astype(bf16)


def split3(values):
    high = values.astype(bf16)
    rest = values - high.astype(f32)
    middle = rest.astype(bf16)
    return high, middle, (rest - middle.astype(f32)).astype(bf16)


def face(f):
    return slice(f * FD, (f + 1) * FD)


def order_of(links_ref, f):
    place = lax.broadcasted_iota(jnp.int32, (FD, FD), 0)
    return jnp.where(place == links_ref[f : f + 1, :], 1.0, 0.0).astype(bf16)


def reorder(order, values):
    high, middle, low = split3(values)
    both = mm(order, jnp.concatenate([high, middle], 1))
    return both[:, :LOADS] + both[:, LOADS:] + mm(order, low)


def pack_kernel(jumps, coupling, links, ids, couple, halves, *packs):
    for f in range(FACES):
        part = coupling[:, face(f)]
        jump = jumps[face(f), :]
        if f % 2:
            order = order_of(links, f)
            jump = -reorder(order, jump)
            high, middle, low = split3(part)
            part = -(mm_t(high, order) + mm_t(middle, order) + mm_t(low, order))
        couple[:, face(f)] = part
        high, low = split(part)
        both = jnp.concatenate([high.astype(f32), low.astype(f32)], 0)
        halves[:, face(f)] = both.astype(bf16)
        packs[f][:FD, :] = jump
        packs[f][FD : FD + CORNERS, :] = part[:, :LOADS]
        packs[f][FD + CORNERS : FD + 2 * CORNERS, :] = part[:, LOADS:]
        packs[f][FD + 2 * CORNERS :, :] = ids[...]


def arrange_kernel(schur, links, weights, schur_out, weights_out, half):
    for f in range(FACES):
        if f % 2:
            order = order_of(links, f)
            half[face(f), :] = (-mm(order, schur[face(f), :])).astype(bf16)
            weights_out[face(f), :] = reorder(order, weights[face(f), :])
        else:
            half[face(f), :] = schur[face(f), :]
            weights_out[face(f), :] = weights[face(f), :]
    for f in range(FACES):
        if f % 2:
            order = order_of(links, f)
            schur_out[:, face(f)] = (-mm_t(half[:, face(f)], order)).astype(bf16)
        else:
            schur_out[:, face(f)] = half[:, face(f)]


def lift_kernel(*refs):
    glued, couple = refs[:2]
    packs = refs[2 : 2 + FACES]
    high, low, rows = refs[2 + FACES :]
    step = pl.program_id(0)
    mask = glued[0, step].astype(f32)
    rows[...] = jnp.zeros_like(rows)
    rows[:CORNERS, :] = couple[...] * mask
    for f in range(FACES):

        @pl.when(step == f)
        def _():
            start = CORNERS * (f + 1)
            rows[start : start + CORNERS, :LOADS] = packs[f][FD : FD + CORNERS, :] * mask
            rows[start : start + CORNERS, LOADS:] = (
                packs[f][FD + CORNERS : FD + 2 * CORNERS, :] * mask
            )

    both = split(rows[...].T)
    high[...] = both[0]
    low[...] = both[1]


def open_face(weights, halves, residual, precond, rounded, state, terms):
    now = weights * residual
    precond[...] = now
    high, low = split(now)
    rounded[...] = high
    state[0:1, :] += 0.5 * jnp.sum(now * residual, 0, keepdims=True)
    terms[...] += mm(halves, jnp.concatenate([high, low], 1))


def place_terms(ids, terms, spread):
    total = terms[:, :LOADS] + terms[:, LOADS:]
    total = total[:CORNERS] + total[CORNERS:]
    spread[...] = jnp.zeros_like(spread)
    for j in range(CORNERS):
        spread[pl.ds(ids[0, j], 1), :] = total[j : j + 1]


def begin_kernel(*refs):
    glued, ids, halves, weights = refs[:4]
    sent = refs[4 : 4 + FACES]
    got = refs[4 + FACES : 4 + 2 * FACES]
    residual, precond, rounded, spread, state, terms = refs[4 + 2 * FACES :]
    step = pl.program_id(0)

    @pl.when(step == 0)
    def _():
        state[...] = jnp.zeros_like(state)
        terms[...] = jnp.zeros_like(terms)

    for f in range(FACES):

        @pl.when(step == f)
        def _():
            residual[...] = glued[0, f].astype(f32) * (sent[f][:FD, :] + got[f][:FD, :])

    open_face(weights[...], halves[...], residual[...], precond, rounded, state, terms)

    @pl.when(step == FACES - 1)
    def _():
        place_terms(ids, terms, spread)


def local_kernel(schur, rounded, precond, state, *refs):
    faces, local, dots = refs[:FACES], refs[FACES], refs[FACES + 1]
    step = pl.program_id(0)
    now = mm(schur[...], rounded[...])
    local[...] = now
    for f in range(FACES):

        @pl.when(step == f)
        def _():
            faces[f][...] = now

    @pl.when(step == 0)
    def _():
        dots[...] = state[...]

    dots[1:2, :] += jnp.sum(now * precond[...], 0, keepdims=True)


def fold_plane_kernel(parts, dots, out):
    total = jnp.sum(parts[...], 0)
    for i in range(LINE):
        out[i, :ROWS, :] = total
        out[i, ROWS:, :] = dots[...]


def fold_line_kernel(parts, out):
    total = jnp.sum(parts[...], 0)
    for i in range(PLANE):
        out[i] = total


def advance_kernel(first, last, *refs):
    glued, ids, near_ids, whole, inverse_high, inverse_low, lift_high, lift_low = refs[:8]
    local, got, refs = refs[8], refs[9 : 9 + FACES], refs[9 + FACES :]
    weights, precond, residual, history = refs[:4]
    refs = refs[4:]
    if not first:
        multipliers, direction, image = refs[:3]
        refs = refs[3:]
    if last:
        links, multipliers_out, residual_out = refs[:3]
    else:
        halves, multipliers_out, residual_out, direction_out, image_out = refs[:5]
        history_out, precond_out, rounded, spread, state = refs[5:10]
    solved, near, near_both, scalars, partner, terms = refs[-6:]
    face_id = pl.program_id(0)

    @pl.when(face_id == 0)
    def _():
        coarse = whole[:, :ROWS, :].reshape(COARSE, LOADS)
        sums = jnp.sum(whole[:, ROWS:, :], 0)
        coarse_high, coarse_low = split(coarse)
        both = mm(inverse_high[...], jnp.concatenate([coarse_high, coarse_low], 1))
        solution_rows = both[:, :LOADS] + both[:, LOADS:] + mm(inverse_low[...], coarse_high)
        solved[...] = solution_rows
        near[...] = jnp.zeros_like(near)
        for j in range(CORNERS * (FACES + 1)):
            near[pl.ds(j, 1), :] = solved[pl.ds(near_ids[0, j], 1), :]
        near_high, near_low = split(near[...])
        near_both[...] = jnp.concatenate([near_high, near_low], 1)
        energy = sums[0:1]
        curvature = sums[1:2] + jnp.sum(coarse * solution_rows, 0, keepdims=True)
        if not first:
            ratio = energy / history[0:1, :]
            curvature = curvature + ratio * (2.0 * sums[2:3] + ratio * history[1:2, :])
            scalars[1:2, :] = ratio
        scalars[0:1, :] = energy / curvature
        if not last:
            history_out[0:1, :] = energy
            history_out[1:2, :] = curvature
            state[...] = jnp.zeros_like(state)
            terms[...] = jnp.zeros_like(terms)

    for f in range(FACES):

        @pl.when(face_id == f)
        def _():
            partner[...] = got[f][...]

    mask = glued[0, face_id].astype(f32)
    lift = mm(lift_high[...], near_both[...])
    lift = lift[:, :LOADS] + lift[:, LOADS:] + mm(lift_low[...], near_both[:, :LOADS])
    now = mask * (local[...] + partner[...]) + lift
    way = precond[...]
    step = scalars[0:1, :]
    if not first:
        ratio = scalars[1:2, :]
        now = now + ratio * image[...]
        way = way + ratio * direction[...]
    move = step * way
    if not first:
        move = multipliers[...] + move
    rest = residual[...] - step * now
    if last:
        multipliers_out[...] = move
        residual_out[...] = rest

        @pl.when(face_id % 2 == 1)
        def _():
            place = lax.broadcasted_iota(jnp.int32, (FD, FD), 0)
            order = jnp.where(place == links[pl.ds(face_id, 1), :], 1.0, 0.0).T.astype(bf16)
            multipliers_out[...] = reorder(order, move)
            residual_out[...] = reorder(order, rest)

    else:
        multipliers_out[...] = move
        residual_out[...] = rest
        direction_out[...] = way
        image_out[...] = now
        open_face(weights[...], halves[...], rest, precond_out, rounded, state, terms)
        state[2:3, :] += 0.5 * jnp.sum(weights[...] * rest * now, 0, keepdims=True)

        @pl.when(face_id == FACES - 1)
        def _():
            place_terms(ids, terms, spread)


def shards(jumps, schur, coupling, coarse_inverse, scaling, glued, matching, corners):
    links = matching[0]
    field = ((DOFS, LOADS), f32, "rows")
    small = ((DOTS, LOADS), f32)
    open_outs = [field, ((DOFS, LOADS), bf16, "rows"), ((COARSE, LOADS), f32), small]
    terms = pltpu.VMEM((2 * CORNERS, 2 * LOADS), f32)
    masks = (glued, "smem")
    own_ids = (corners, "smem")

    ids_row = jnp.pad(corners.astype(f32), ((0, 7), (0, LOADS - CORNERS)))
    couple, halves, *sent = call(
        pack_kernel,
        1,
        [((CORNERS, DOFS), f32), ((2 * CORNERS, DOFS), bf16)] + [((PACKED, LOADS), f32)] * FACES,
        [jumps[0], coupling[0], links, ids_row],
    )
    halves = (halves, "columns")
    got = swap_faces(sent)
    schur_block, weights = call(
        arrange_kernel,
        1,
        [((DOFS, DOFS), bf16), ((DOFS, LOADS), f32)],
        [schur[0], links, jnp.broadcast_to(scaling[0][:, None], (DOFS, LOADS))],
        scratch=[pltpu.VMEM((DOFS, DOFS), bf16)],
        flops=4 * DOFS * DOFS * FD,
    )
    weights = (weights, "rows")
    residual, precond, rounded, spread, state = call(
        begin_kernel,
        FACES,
        [field] + open_outs,
        [masks, own_ids, halves, weights, *sent, *got],
        scratch=[terms],
    )
    lift_high, lift_low = call(
        lift_kernel,
        FACES,
        [((DOFS, NEAR), bf16, "rows")] * 2,
        [masks, (couple, "columns"), *got],
        scratch=[pltpu.VMEM((NEAR, FD), f32)],
    )
    near_ids = jnp.concatenate(
        [corners] + [g[FD + 2 * CORNERS :][:1, :CORNERS].astype(jnp.int32) for g in got], 1
    )
    kept = lax.reduce_precision(coarse_inverse, 8, 7)
    inverse_high, inverse_low = kept.astype(bf16), (coarse_inverse - kept).astype(bf16)

    multipliers = direction = image = history = None
    for iteration in range(ITERS):
        first, last = iteration == 0, iteration + 1 == ITERS
        parts = lax.all_to_all(
            spread.reshape(PLANE, ROWS, LOADS), "sub", 0, 0, axis_index_groups=PLANES
        )
        *faces, local, dots = call(
            local_kernel,
            FACES,
            [((FD, LOADS), f32)] * FACES + [field, small],
            [(schur_block, "rows"), rounded, (precond, "rows"), state],
            flops=2 * DOFS * DOFS * LOADS,
        )
        received = swap_faces(faces)
        (lines,) = call(fold_plane_kernel, 1, [((LINE, ROWS + DOTS, LOADS), f32)], [parts, dots])
        lines = lax.all_to_all(lines, "sub", 0, 0, axis_index_groups=LINES)
        (whole,) = call(fold_line_kernel, 1, [((PLANE, ROWS + DOTS, LOADS), f32)], [lines])
        whole = lax.all_to_all(whole, "sub", 0, 0, axis_index_groups=PLANES)
        inputs = [masks, own_ids, (near_ids, "smem"), whole, inverse_high, inverse_low]
        inputs += [(lift_high, "rows"), (lift_low, "rows"), (local, "rows"), *received]
        inputs += [weights, (precond, "rows"), (residual, "rows"), state if first else history]
        if not first:
            inputs += [(multipliers, "rows"), (direction, "rows"), (image, "rows")]
        inputs += [links if last else halves]
        outs = [field, field]
        if not last:
            outs += [field, field, small] + open_outs
        results = call(
            functools.partial(advance_kernel, first, last),
            FACES,
            outs,
            inputs,
            scratch=[
                pltpu.VMEM((COARSE, LOADS), f32),
                pltpu.VMEM((NEAR, LOADS), f32),
                pltpu.VMEM((NEAR, 2 * LOADS), bf16),
                pltpu.VMEM((8, LOADS), f32),
                pltpu.VMEM((FD, LOADS), f32),
                terms,
            ],
        )
        multipliers, residual = results[:2]
        if not last:
            direction, image, history, precond, rounded, spread, state = results[2:]
    return (multipliers[None], residual[None])


def solution(mesh):
    return jax.shard_map(
        shards,
        mesh=mesh,
        in_specs=(
            P("sub", None, None),
            P("sub", None, None),
            P("sub", None, None),
            P(),
            P("sub", None),
            P("sub", None),
            P("sub", None, None),
            P("sub", None),
        ),
        out_specs=(P("sub", None, None), P("sub", None, None)),
        check_vma=False,
    )
```

```python
import functools

import jax
import jax.numpy as jnp
import numpy as np
from jax import lax
from jax.experimental import pallas as pl
from jax.experimental.pallas import tpu as pltpu
from jax.sharding import PartitionSpec as P

ITERS = 5
STRIDES = (1, 4, 16)
GRID = (4, 4, 16)
NSUB = 256
FACES = 6
FD = 256
DOFS = FACES * FD
LOADS = 128
CORNERS = 24
COARSE = 768
NEAR = 256
DOTS = 8
PACKED = FD + 2 * CORNERS + 8
PLACES = np.arange(NSUB).reshape(4, 8, 8)
PLANES = PLACES.transpose(1, 0, 2).reshape(8, 32).tolist()
LINES = PLACES.transpose(0, 2, 1).reshape(32, 8).tolist()
PLANE = 32
LINE = 8
ROWS = COARSE // PLANE
f32 = jnp.float32
bf16 = jnp.bfloat16


def route(direction, sign):
    stride, extent = STRIDES[direction], GRID[direction]
    pairs = []
    for i in range(NSUB):
        place = i // stride % extent
        if 0 <= place + sign < extent:
            pairs.append((i, i + sign * stride))
    return pairs


UP = [route(d, 1) for d in range(3)]
DOWN = [route(d, -1) for d in range(3)]


def swap_faces(blocks):
    received = [None] * FACES
    for d in range(3):
        received[2 * d] = lax.ppermute(blocks[2 * d + 1], "sub", DOWN[d])
    for d in range(3):
        received[2 * d + 1] = lax.ppermute(blocks[2 * d], "sub", UP[d])
    return received


def block_of(shape, kind):
    if kind == "smem":
        return pl.BlockSpec(memory_space=pltpu.SMEM)
    if kind == "rows":
        return pl.BlockSpec((FD, shape[1]), lambda f: (f, 0))
    if kind == "columns":
        return pl.BlockSpec((shape[0], FD), lambda f: (0, f))
    return pl.BlockSpec(shape, lambda f: (0,) * len(shape))


def call(kernel, steps, outs, inputs, scratch=(), flops=0):
    inputs = [x if isinstance(x, tuple) else (x, "whole") for x in inputs]
    outs = [x if len(x) == 3 else (*x, "whole") for x in outs]
    size = sum(int(np.prod(s)) * jnp.dtype(t).itemsize for s, t, _ in outs)
    size += sum(x.size * x.dtype.itemsize for x, _ in inputs)
    return pl.pallas_call(
        kernel,
        grid=(steps,),
        out_shape=[jax.ShapeDtypeStruct(s, t) for s, t, _ in outs],
        in_specs=[block_of(x.shape, kind) for x, kind in inputs],
        out_specs=[block_of(s, kind) for s, _, kind in outs],
        scratch_shapes=list(scratch),
        compiler_params=pltpu.CompilerParams(vmem_limit_bytes=56 * 2**20),
        cost_estimate=pl.CostEstimate(flops=flops, bytes_accessed=size, transcendentals=0),
    )(*[x for x, _ in inputs])


def mm(a, b):
    return lax.dot_general(a, b, (((1,), (0,)), ((), ())), preferred_element_type=f32)


def mm_t(a, b):
    return lax.dot_general(a, b, (((1,), (1,)), ((), ())), preferred_element_type=f32)


def split(values):
    high = values.astype(bf16)
    return high, (values - high.astype(f32)).astype(bf16)


def split3(values):
    high = values.astype(bf16)
    rest = values - high.astype(f32)
    middle = rest.astype(bf16)
    return high, middle, (rest - middle.astype(f32)).astype(bf16)


def face(f):
    return slice(f * FD, (f + 1) * FD)


def order_of(links_ref, f):
    place = lax.broadcasted_iota(jnp.int32, (FD, FD), 0)
    return jnp.where(place == links_ref[f : f + 1, :], 1.0, 0.0).astype(bf16)


def reorder(order, values):
    high, middle, low = split3(values)
    both = mm(order, jnp.concatenate([high, middle], 1))
    return both[:, :LOADS] + both[:, LOADS:] + mm(order, low)


def pack_kernel(jumps, coupling, links, ids, couple, halves, *packs):
    for f in range(FACES):
        part = coupling[:, face(f)]
        jump = jumps[face(f), :]
        if f % 2:
            order = order_of(links, f)
            jump = -reorder(order, jump)
            high, middle, low = split3(part)
            part = -(mm_t(high, order) + mm_t(middle, order) + mm_t(low, order))
        couple[:, face(f)] = part
        high, low = split(part)
        both = jnp.concatenate([high.astype(f32), low.astype(f32)], 0)
        halves[:, face(f)] = both.astype(bf16)
        packs[f][:FD, :] = jump
        packs[f][FD : FD + CORNERS, :] = part[:, :LOADS]
        packs[f][FD + CORNERS : FD + 2 * CORNERS, :] = part[:, LOADS:]
        packs[f][FD + 2 * CORNERS :, :] = ids[...]


def arrange_kernel(schur, links, weights, schur_out, weights_out, half):
    for f in range(FACES):
        if f % 2:
            order = order_of(links, f)
            half[face(f), :] = (-mm(order, schur[face(f), :])).astype(bf16)
            weights_out[face(f), :] = reorder(order, weights[face(f), :])
        else:
            half[face(f), :] = schur[face(f), :]
            weights_out[face(f), :] = weights[face(f), :]
    for f in range(FACES):
        if f % 2:
            order = order_of(links, f)
            schur_out[:, face(f)] = (-mm_t(half[:, face(f)], order)).astype(bf16)
        else:
            schur_out[:, face(f)] = half[:, face(f)]


def lift_kernel(*refs):
    glued, couple = refs[:2]
    packs = refs[2 : 2 + FACES]
    high, low, rows = refs[2 + FACES :]
    step = pl.program_id(0)
    mask = glued[0, step].astype(f32)
    rows[...] = jnp.zeros_like(rows)
    rows[:CORNERS, :] = couple[...] * mask
    for f in range(FACES):

        @pl.when(step == f)
        def _():
            start = CORNERS * (f + 1)
            rows[start : start + CORNERS, :LOADS] = packs[f][FD : FD + CORNERS, :] * mask
            rows[start : start + CORNERS, LOADS:] = (
                packs[f][FD + CORNERS : FD + 2 * CORNERS, :] * mask
            )

    both = split(rows[...].T)
    high[...] = both[0]
    low[...] = both[1]


def open_face(weights, halves, residual, precond, rounded, state, terms):
    now = weights * residual
    precond[...] = now
    high, low = split(now)
    rounded[...] = high
    state[0:1, :] += 0.5 * jnp.sum(now * residual, 0, keepdims=True)
    terms[...] += mm(halves, jnp.concatenate([high, low], 1))


def place_terms(ids, terms, spread):
    total = terms[:, :LOADS] + terms[:, LOADS:]
    total = total[:CORNERS] + total[CORNERS:]
    spread[...] = jnp.zeros_like(spread)
    for j in range(CORNERS):
        spread[pl.ds(ids[0, j], 1), :] = total[j : j + 1]


def begin_kernel(*refs):
    glued, ids, halves, weights = refs[:4]
    sent = refs[4 : 4 + FACES]
    got = refs[4 + FACES : 4 + 2 * FACES]
    residual, precond, rounded, spread, state, terms = refs[4 + 2 * FACES :]
    step = pl.program_id(0)

    @pl.when(step == 0)
    def _():
        state[...] = jnp.zeros_like(state)
        terms[...] = jnp.zeros_like(terms)

    for f in range(FACES):

        @pl.when(step == f)
        def _():
            residual[...] = glued[0, f].astype(f32) * (sent[f][:FD, :] + got[f][:FD, :])

    open_face(weights[...], halves[...], residual[...], precond, rounded, state, terms)

    @pl.when(step == FACES - 1)
    def _():
        place_terms(ids, terms, spread)


def local_kernel(schur, rounded, precond, state, *refs):
    faces, local, dots = refs[:FACES], refs[FACES], refs[FACES + 1]
    step = pl.program_id(0)
    now = mm(schur[...], rounded[...])
    local[...] = now
    for f in range(FACES):

        @pl.when(step == f)
        def _():
            faces[f][...] = now

    @pl.when(step == 0)
    def _():
        dots[...] = state[...]

    dots[1:2, :] += jnp.sum(now * precond[...], 0, keepdims=True)


def fold_plane_kernel(parts, dots, out):
    total = jnp.sum(parts[...], 0)
    for i in range(LINE):
        out[i, :ROWS, :] = total
        out[i, ROWS:, :] = dots[...]


def fold_line_kernel(parts, out):
    total = jnp.sum(parts[...], 0)
    for i in range(PLANE):
        out[i] = total


def advance_kernel(first, last, *refs):
    glued, ids, near_ids, whole, inverse_high, inverse_low, lift_high, lift_low = refs[:8]
    local, got, refs = refs[8], refs[9 : 9 + FACES], refs[9 + FACES :]
    weights, precond, residual, history = refs[:4]
    refs = refs[4:]
    if not first:
        multipliers, direction, image = refs[:3]
        refs = refs[3:]
    if last:
        links, multipliers_out, residual_out = refs[:3]
    else:
        halves, multipliers_out, residual_out, direction_out, image_out = refs[:5]
        history_out, precond_out, rounded, spread, state = refs[5:10]
    solved, near, near_both, scalars, partner, terms = refs[-6:]
    face_id = pl.program_id(0)

    @pl.when(face_id == 0)
    def _():
        coarse = whole[:, :ROWS, :].reshape(COARSE, LOADS)
        sums = jnp.sum(whole[:, ROWS:, :], 0)
        coarse_high, coarse_low = split(coarse)
        both = mm(inverse_high[...], jnp.concatenate([coarse_high, coarse_low], 1))
        solution_rows = both[:, :LOADS] + both[:, LOADS:] + mm(inverse_low[...], coarse_high)
        solved[...] = solution_rows
        near[...] = jnp.zeros_like(near)
        for j in range(CORNERS * (FACES + 1)):
            near[pl.ds(j, 1), :] = solved[pl.ds(near_ids[0, j], 1), :]
        near_high, near_low = split(near[...])
        near_both[...] = jnp.concatenate([near_high, near_low], 1)
        energy = sums[0:1]
        curvature = sums[1:2] + jnp.sum(coarse * solution_rows, 0, keepdims=True)
        if not first:
            ratio = energy / history[0:1, :]
            curvature = curvature + ratio * (2.0 * sums[2:3] + ratio * history[1:2, :])
            scalars[1:2, :] = ratio
        scalars[0:1, :] = energy / curvature
        if not last:
            history_out[0:1, :] = energy
            history_out[1:2, :] = curvature
            state[...] = jnp.zeros_like(state)
            terms[...] = jnp.zeros_like(terms)

    for f in range(FACES):

        @pl.when(face_id == f)
        def _():
            partner[...] = got[f][...]

    mask = glued[0, face_id].astype(f32)
    lift = mm(lift_high[...], near_both[...])
    lift = lift[:, :LOADS] + lift[:, LOADS:] + mm(lift_low[...], near_both[:, :LOADS])
    now = mask * (local[...] + partner[...]) + lift
    way = precond[...]
    step = scalars[0:1, :]
    if not first:
        ratio = scalars[1:2, :]
        now = now + ratio * image[...]
        way = way + ratio * direction[...]
    move = step * way
    if not first:
        move = multipliers[...] + move
    rest = residual[...] - step * now
    if last:
        multipliers_out[...] = move
        residual_out[...] = rest

        @pl.when(face_id % 2 == 1)
        def _():
            place = lax.broadcasted_iota(jnp.int32, (FD, FD), 0)
            order = jnp.where(place == links[pl.ds(face_id, 1), :], 1.0, 0.0).T.astype(bf16)
            multipliers_out[...] = reorder(order, move)
            residual_out[...] = reorder(order, rest)

    else:
        multipliers_out[...] = move
        residual_out[...] = rest
        direction_out[...] = way
        image_out[...] = now
        open_face(weights[...], halves[...], rest, precond_out, rounded, state, terms)
        state[2:3, :] += 0.5 * jnp.sum(weights[...] * rest * now, 0, keepdims=True)

        @pl.when(face_id == FACES - 1)
        def _():
            place_terms(ids, terms, spread)


def shards(jumps, schur, coupling, coarse_inverse, scaling, glued, matching, corners):
    links = matching[0]
    field = ((DOFS, LOADS), f32, "rows")
    small = ((DOTS, LOADS), f32)
    open_outs = [field, ((DOFS, LOADS), bf16, "rows"), ((COARSE, LOADS), f32), small]
    terms = pltpu.VMEM((2 * CORNERS, 2 * LOADS), f32)
    masks = (glued, "smem")
    own_ids = (corners, "smem")

    ids_row = jnp.pad(corners.astype(f32), ((0, 7), (0, LOADS - CORNERS)))
    couple, halves, *sent = call(
        pack_kernel,
        1,
        [((CORNERS, DOFS), f32), ((2 * CORNERS, DOFS), bf16)] + [((PACKED, LOADS), f32)] * FACES,
        [jumps[0], coupling[0], links, ids_row],
    )
    halves = (halves, "columns")
    got = swap_faces(sent)
    schur_block, weights = call(
        arrange_kernel,
        1,
        [((DOFS, DOFS), bf16), ((DOFS, LOADS), f32)],
        [schur[0], links, jnp.broadcast_to(scaling[0][:, None], (DOFS, LOADS))],
        scratch=[pltpu.VMEM((DOFS, DOFS), bf16)],
        flops=4 * DOFS * DOFS * FD,
    )
    weights = (weights, "rows")
    residual, precond, rounded, spread, state = call(
        begin_kernel,
        FACES,
        [field] + open_outs,
        [masks, own_ids, halves, weights, *sent, *got],
        scratch=[terms],
    )
    lift_high, lift_low = call(
        lift_kernel,
        FACES,
        [((DOFS, NEAR), bf16, "rows")] * 2,
        [masks, (couple, "columns"), *got],
        scratch=[pltpu.VMEM((NEAR, FD), f32)],
    )
    near_ids = jnp.concatenate(
        [corners] + [g[FD + 2 * CORNERS :][:1, :CORNERS].astype(jnp.int32) for g in got], 1
    )
    kept = lax.reduce_precision(coarse_inverse, 8, 7)
    inverse_high, inverse_low = kept.astype(bf16), (coarse_inverse - kept).astype(bf16)

    multipliers = direction = image = history = None
    for iteration in range(ITERS):
        first, last = iteration == 0, iteration + 1 == ITERS
        parts = lax.all_to_all(
            spread.reshape(PLANE, ROWS, LOADS), "sub", 0, 0, axis_index_groups=PLANES
        )
        *faces, local, dots = call(
            local_kernel,
            FACES,
            [((FD, LOADS), f32)] * FACES + [field, small],
            [(schur_block, "rows"), rounded, (precond, "rows"), state],
            flops=2 * DOFS * DOFS * LOADS,
        )
        received = swap_faces(faces)
        (lines,) = call(fold_plane_kernel, 1, [((LINE, ROWS + DOTS, LOADS), f32)], [parts, dots])
        lines = lax.all_to_all(lines, "sub", 0, 0, axis_index_groups=LINES)
        (whole,) = call(fold_line_kernel, 1, [((PLANE, ROWS + DOTS, LOADS), f32)], [lines])
        whole = lax.all_to_all(whole, "sub", 0, 0, axis_index_groups=PLANES)
        inputs = [masks, own_ids, (near_ids, "smem"), whole, inverse_high, inverse_low]
        inputs += [(lift_high, "rows"), (lift_low, "rows"), (local, "rows"), *received]
        inputs += [weights, (precond, "rows"), (residual, "rows"), state if first else history]
        if not first:
            inputs += [(multipliers, "rows"), (direction, "rows"), (image, "rows")]
        inputs += [links if last else halves]
        outs = [field, field]
        if not last:
            outs += [field, field, small] + open_outs
        results = call(
            functools.partial(advance_kernel, first, last),
            FACES,
            outs,
            inputs,
            scratch=[
                pltpu.VMEM((COARSE, LOADS), f32),
                pltpu.VMEM((NEAR, LOADS), f32),
                pltpu.VMEM((NEAR, 2 * LOADS), bf16),
                pltpu.VMEM((8, LOADS), f32),
                pltpu.VMEM((FD, LOADS), f32),
                terms,
            ],
        )
        multipliers, residual = results[:2]
        if not last:
            direction, image, history, precond, rounded, spread, state = results[2:]
    return (multipliers[None], residual[None])


def solution(mesh):
    return jax.shard_map(
        shards,
        mesh=mesh,
        in_specs=(
            P("sub", None, None),
            P("sub", None, None),
            P("sub", None, None),
            P(),
            P("sub", None),
            P("sub", None),
            P("sub", None, None),
            P("sub", None),
        ),
        out_specs=(P("sub", None, None), P("sub", None, None)),
        check_vma=False,
    )
```

```python
import functools

import jax
import jax.numpy as jnp
import numpy as np
from jax import lax
from jax.experimental import pallas as pl
from jax.experimental.pallas import tpu as pltpu
from jax.sharding import PartitionSpec as P

ITERS = 5
STRIDES = (1, 4, 16)
GRID = (4, 4, 16)
NSUB = 256
FACES = 6
FD = 256
DOFS = FACES * FD
LOADS = 128
CORNERS = 24
COARSE = 768
NEAR = 256
DOTS = 8
TURN = (0, 2, 4, 1, 3, 5)
EARLY = (0, 1, 2)
PACKED = FD + 2 * CORNERS + 8
PLACES = np.arange(NSUB).reshape(4, 8, 8)
PLANES = PLACES.transpose(1, 0, 2).reshape(8, 32).tolist()
LINES = PLACES.transpose(0, 2, 1).reshape(32, 8).tolist()
PLANE = 32
LINE = 8
ROWS = COARSE // PLANE
f32 = jnp.float32
bf16 = jnp.bfloat16


def route(direction, sign):
    stride, extent = STRIDES[direction], GRID[direction]
    pairs = []
    for i in range(NSUB):
        place = i // stride % extent
        if 0 <= place + sign < extent:
            pairs.append((i, i + sign * stride))
    return pairs


UP = [route(d, 1) for d in range(3)]
DOWN = [route(d, -1) for d in range(3)]


def swap_faces(blocks):
    return [
        lax.ppermute(blocks[f ^ 1], "sub", UP[f // 2] if f % 2 else DOWN[f // 2]) for f in TURN
    ]


def block_of(shape, kind):
    if kind == "smem":
        return pl.BlockSpec(memory_space=pltpu.SMEM)
    if kind == "held":
        return pl.BlockSpec(memory_space=pl.ANY)
    if kind == "rows":
        return pl.BlockSpec((FD, shape[1]), lambda f: (f, 0))
    if kind == "columns":
        return pl.BlockSpec((shape[0], FD), lambda f: (0, f))
    return pl.BlockSpec(shape, lambda f: (0,) * len(shape))


def call(kernel, steps, outs, inputs, scratch=(), flops=0, alias={}):
    inputs = [x if isinstance(x, tuple) else (x, "whole") for x in inputs]
    outs = [x if len(x) == 3 else (*x, "whole") for x in outs]
    size = sum(int(np.prod(s)) * jnp.dtype(t).itemsize for s, t, _ in outs)
    size += sum(x.size * x.dtype.itemsize for x, _ in inputs)
    return pl.pallas_call(
        kernel,
        grid=(steps,),
        out_shape=[jax.ShapeDtypeStruct(s, t) for s, t, _ in outs],
        in_specs=[block_of(x.shape, kind) for x, kind in inputs],
        out_specs=[block_of(s, kind) for s, _, kind in outs],
        scratch_shapes=list(scratch),
        input_output_aliases=alias,
        compiler_params=pltpu.CompilerParams(vmem_limit_bytes=56 * 2**20),
        cost_estimate=pl.CostEstimate(flops=flops, bytes_accessed=size, transcendentals=0),
    )(*[x for x, _ in inputs])


def mm(a, b):
    return lax.dot_general(a, b, (((1,), (0,)), ((), ())), preferred_element_type=f32)


def mm_t(a, b):
    return lax.dot_general(a, b, (((1,), (1,)), ((), ())), preferred_element_type=f32)


def split(values):
    high = values.astype(bf16)
    return high, (values - high.astype(f32)).astype(bf16)


def split3(values):
    high = values.astype(bf16)
    rest = values - high.astype(f32)
    middle = rest.astype(bf16)
    return high, middle, (rest - middle.astype(f32)).astype(bf16)


def face(f):
    return slice(f * FD, (f + 1) * FD)


def order_of(links_ref, f):
    place = lax.broadcasted_iota(jnp.int32, (FD, FD), 0)
    return jnp.where(place == links_ref[f : f + 1, :], 1.0, 0.0).astype(bf16)


def reorder(order, values):
    high, middle, low = split3(values)
    both = mm(order, jnp.concatenate([high, middle], 1))
    return both[:, :LOADS] + both[:, LOADS:] + mm(order, low)


def pack_kernel(jumps, coupling, links, ids, couple, halves, *packs):
    for f in range(FACES):
        part = coupling[:, face(f)]
        jump = jumps[face(f), :]
        if f % 2:
            order = order_of(links, f)
            jump = -reorder(order, jump)
            high, middle, low = split3(part)
            part = -(mm_t(high, order) + mm_t(middle, order) + mm_t(low, order))
        couple[:, face(f)] = part
        high, low = split(part)
        both = jnp.concatenate([high.astype(f32), low.astype(f32)], 0)
        halves[:, face(f)] = both.astype(bf16)
        packs[f][:FD, :] = jump
        packs[f][FD : FD + CORNERS, :] = part[:, :LOADS]
        packs[f][FD + CORNERS : FD + 2 * CORNERS, :] = part[:, LOADS:]
        packs[f][FD + 2 * CORNERS :, :] = ids[...]


def arrange_kernel(schur, links, weights, schur_out, weights_out, half):
    for f in range(FACES):
        if f % 2:
            order = order_of(links, f)
            half[face(f), :] = (-mm(order, schur[face(f), :])).astype(bf16)
            weights_out[face(f), :] = reorder(order, weights[face(f), :])
        else:
            half[face(f), :] = schur[face(f), :]
            weights_out[face(f), :] = weights[face(f), :]
    for f in range(FACES):
        if f % 2:
            order = order_of(links, f)
            schur_out[:, face(f)] = (-mm_t(half[:, face(f)], order)).astype(bf16)
        else:
            schur_out[:, face(f)] = half[:, face(f)]


def lift_kernel(*refs):
    glued, couple = refs[:2]
    packs = [refs[2 + TURN.index(f)] for f in range(FACES)]
    high, low, rows = refs[2 + FACES :]
    step = pl.program_id(0)
    mask = glued[0, step].astype(f32)
    rows[...] = jnp.zeros_like(rows)
    rows[:CORNERS, :] = couple[...] * mask
    for f in range(FACES):

        @pl.when(step == f)
        def _():
            start = CORNERS * (f + 1)
            rows[start : start + CORNERS, :LOADS] = packs[f][FD : FD + CORNERS, :] * mask
            rows[start : start + CORNERS, LOADS:] = (
                packs[f][FD + CORNERS : FD + 2 * CORNERS, :] * mask
            )

    both = split(rows[...].T)
    high[...] = both[0]
    low[...] = both[1]


def open_face(weights, halves, residual, precond, rounded, state, terms):
    now = weights * residual
    precond[...] = now
    high, low = split(now)
    rounded[...] = high
    state[0:1, :] += 0.5 * jnp.sum(now * residual, 0, keepdims=True)
    terms[...] += mm(halves, jnp.concatenate([high, low], 1))


def place_terms(ids, terms, spread):
    total = terms[:, :LOADS] + terms[:, LOADS:]
    total = total[:CORNERS] + total[CORNERS:]
    spread[...] = jnp.zeros_like(spread)
    for j in range(CORNERS):
        spread[pl.ds(ids[0, j], 1), :] = total[j : j + 1]


def begin_kernel(*refs):
    glued, ids, halves, weights = refs[:4]
    sent = refs[4 : 4 + FACES]
    got = [refs[4 + FACES + TURN.index(f)] for f in range(FACES)]
    residual, precond, rounded, spread, state, terms = refs[4 + 2 * FACES :]
    step = pl.program_id(0)

    @pl.when(step == 0)
    def _():
        state[...] = jnp.zeros_like(state)
        terms[...] = jnp.zeros_like(terms)

    for f in range(FACES):

        @pl.when(step == f)
        def _():
            residual[...] = glued[0, f].astype(f32) * (sent[f][:FD, :] + got[f][:FD, :])

    open_face(weights[...], halves[...], residual[...], precond, rounded, state, terms)

    @pl.when(step == FACES - 1)
    def _():
        place_terms(ids, terms, spread)


def local_kernel(schur, rounded, precond, state, *refs):
    faces, local, dots = refs[:FACES], refs[FACES], refs[FACES + 1]
    step = pl.program_id(0)
    now = mm(schur[...], rounded[...])
    local[...] = now
    for f in range(FACES):

        @pl.when(step == f)
        def _():
            faces[f][...] = now

    @pl.when(step == 0)
    def _():
        dots[...] = state[...]

    dots[1:2, :] += jnp.sum(now * precond[...], 0, keepdims=True)


def fold_plane_kernel(parts, dots, out):
    total = jnp.sum(parts[...], 0)
    for i in range(LINE):
        out[i, :ROWS, :] = total
        out[i, ROWS:, :] = dots[...]


def fold_line_kernel(parts, *refs):
    out = refs[-1]
    total = jnp.sum(parts[...], 0)
    for i in range(PLANE):
        out[i] = total


def advance_kernel(first, last, *refs):
    glued, ids, near_ids, whole, inverse_high, inverse_low, lift_high, lift_low = refs[:8]
    local, got, refs = refs[8], [refs[9 + TURN.index(f)] for f in range(FACES)], refs[9 + FACES :]
    weights, precond, residual, history = refs[:4]
    refs = refs[4:]
    if not first:
        multipliers, direction, image = refs[:3]
        refs = refs[3:]
    if last:
        links, multipliers_out, residual_out = refs[:3]
    else:
        halves, multipliers_out, residual_out, direction_out, image_out = refs[:5]
        history_out, precond_out, rounded, spread, state = refs[5:10]
    solved, near, near_both, scalars, partner, terms = refs[-6:]
    face_id = pl.program_id(0)

    @pl.when(face_id == 0)
    def _():
        coarse = whole[:, :ROWS, :].reshape(COARSE, LOADS)
        sums = jnp.sum(whole[:, ROWS:, :], 0)
        coarse_high, coarse_low = split(coarse)
        both = mm(inverse_high[...], jnp.concatenate([coarse_high, coarse_low], 1))
        solution_rows = both[:, :LOADS] + both[:, LOADS:] + mm(inverse_low[...], coarse_high)
        solved[...] = solution_rows
        near[...] = jnp.zeros_like(near)
        for j in range(CORNERS * (FACES + 1)):
            near[pl.ds(j, 1), :] = solved[pl.ds(near_ids[0, j], 1), :]
        near_high, near_low = split(near[...])
        near_both[...] = jnp.concatenate([near_high, near_low], 1)
        energy = sums[0:1]
        curvature = sums[1:2] + jnp.sum(coarse * solution_rows, 0, keepdims=True)
        if not first:
            ratio = energy / history[0:1, :]
            curvature = curvature + ratio * (2.0 * sums[2:3] + ratio * history[1:2, :])
            scalars[1:2, :] = ratio
        scalars[0:1, :] = energy / curvature
        if not last:
            history_out[0:1, :] = energy
            history_out[1:2, :] = curvature
            state[...] = jnp.zeros_like(state)
            terms[...] = jnp.zeros_like(terms)

    for f in range(FACES):

        @pl.when(face_id == f)
        def _():
            partner[...] = got[f][...]

    mask = glued[0, face_id].astype(f32)
    lift = mm(lift_high[...], near_both[...])
    lift = lift[:, :LOADS] + lift[:, LOADS:] + mm(lift_low[...], near_both[:, :LOADS])
    now = mask * (local[...] + partner[...]) + lift
    way = precond[...]
    step = scalars[0:1, :]
    if not first:
        ratio = scalars[1:2, :]
        now = now + ratio * image[...]
        way = way + ratio * direction[...]
    move = step * way
    if not first:
        move = multipliers[...] + move
    rest = residual[...] - step * now
    if last:
        multipliers_out[...] = move
        residual_out[...] = rest

        @pl.when(face_id % 2 == 1)
        def _():
            place = lax.broadcasted_iota(jnp.int32, (FD, FD), 0)
            order = jnp.where(place == links[pl.ds(face_id, 1), :], 1.0, 0.0).T.astype(bf16)
            multipliers_out[...] = reorder(order, move)
            residual_out[...] = reorder(order, rest)

    else:
        multipliers_out[...] = move
        residual_out[...] = rest
        direction_out[...] = way
        image_out[...] = now
        open_face(weights[...], halves[...], rest, precond_out, rounded, state, terms)
        state[2:3, :] += 0.5 * jnp.sum(weights[...] * rest * now, 0, keepdims=True)

        @pl.when(face_id == FACES - 1)
        def _():
            place_terms(ids, terms, spread)


def shards(jumps, schur, coupling, coarse_inverse, scaling, glued, matching, corners):
    links = matching[0]
    field = ((DOFS, LOADS), f32, "rows")
    small = ((DOTS, LOADS), f32)
    open_outs = [field, ((DOFS, LOADS), bf16, "rows"), ((COARSE, LOADS), f32), small]
    terms = pltpu.VMEM((2 * CORNERS, 2 * LOADS), f32)
    masks = (glued, "smem")
    own_ids = (corners, "smem")

    ids_row = jnp.pad(corners.astype(f32), ((0, 7), (0, LOADS - CORNERS)))
    couple, halves, *sent = call(
        pack_kernel,
        1,
        [((CORNERS, DOFS), f32), ((2 * CORNERS, DOFS), bf16)] + [((PACKED, LOADS), f32)] * FACES,
        [jumps[0], coupling[0], links, ids_row],
    )
    halves = (halves, "columns")
    got = swap_faces(sent)
    schur_block, weights = call(
        arrange_kernel,
        1,
        [((DOFS, DOFS), bf16), ((DOFS, LOADS), f32)],
        [schur[0], links, jnp.broadcast_to(scaling[0][:, None], (DOFS, LOADS))],
        scratch=[pltpu.VMEM((DOFS, DOFS), bf16)],
        flops=4 * DOFS * DOFS * FD,
    )
    weights = (weights, "rows")
    residual, precond, rounded, spread, state = call(
        begin_kernel,
        FACES,
        [field] + open_outs,
        [masks, own_ids, halves, weights, *sent, *got],
        scratch=[terms],
    )
    lift_high, lift_low = call(
        lift_kernel,
        FACES,
        [((DOFS, NEAR), bf16, "rows")] * 2,
        [masks, (couple, "columns"), *got],
        scratch=[pltpu.VMEM((NEAR, FD), f32)],
    )
    near_ids = jnp.concatenate(
        [corners]
        + [
            got[TURN.index(f)][FD + 2 * CORNERS :][:1, :CORNERS].astype(jnp.int32)
            for f in range(FACES)
        ],
        1,
    )
    kept = lax.reduce_precision(coarse_inverse, 8, 7)
    inverse_high, inverse_low = kept.astype(bf16), (coarse_inverse - kept).astype(bf16)

    multipliers = direction = image = history = None
    for iteration in range(ITERS):
        first, last = iteration == 0, iteration + 1 == ITERS
        parts = lax.all_to_all(
            spread.reshape(PLANE, ROWS, LOADS), "sub", 0, 0, axis_index_groups=PLANES
        )
        *faces, local, dots = call(
            local_kernel,
            FACES,
            [((FD, LOADS), f32)] * FACES + [field, small],
            [(schur_block, "rows"), rounded, (precond, "rows"), state],
            flops=2 * DOFS * DOFS * LOADS,
        )
        received = swap_faces(faces)
        early = [(received[TURN.index(f)], "held") for f in EARLY]
        (lines,) = call(fold_plane_kernel, 1, [((LINE, ROWS + DOTS, LOADS), f32)], [parts, dots])
        lines = lax.all_to_all(lines, "sub", 0, 0, axis_index_groups=LINES)
        (whole,) = call(fold_line_kernel, 1, [((PLANE, ROWS + DOTS, LOADS), f32)], [lines, *early])
        whole = lax.all_to_all(whole, "sub", 0, 0, axis_index_groups=PLANES)
        inputs = [masks, own_ids, (near_ids, "smem"), whole, inverse_high, inverse_low]
        inputs += [(lift_high, "rows"), (lift_low, "rows"), (local, "rows"), *received]
        inputs += [weights, (precond, "rows"), (residual, "rows"), state if first else history]
        if not first:
            inputs += [(multipliers, "rows"), (direction, "rows"), (image, "rows")]
        inputs += [links if last else halves]
        outs = [field, field]
        if not last:
            outs += [field, field, small] + open_outs
        results = call(
            functools.partial(advance_kernel, first, last),
            FACES,
            outs,
            inputs,
            scratch=[
                pltpu.VMEM((COARSE, LOADS), f32),
                pltpu.VMEM((NEAR, LOADS), f32),
                pltpu.VMEM((NEAR, 2 * LOADS), bf16),
                pltpu.VMEM((8, LOADS), f32),
                pltpu.VMEM((FD, LOADS), f32),
                terms,
            ],
        )
        multipliers, residual = results[:2]
        if not last:
            direction, image, history, precond, rounded, spread, state = results[2:]
    return (multipliers[None], residual[None])


def solution(mesh):
    return jax.shard_map(
        shards,
        mesh=mesh,
        in_specs=(
            P("sub", None, None),
            P("sub", None, None),
            P("sub", None, None),
            P(),
            P("sub", None),
            P("sub", None),
            P("sub", None, None),
            P("sub", None),
        ),
        out_specs=(P("sub", None, None), P("sub", None, None)),
        check_vma=False,
    )
```

```python
import functools

import jax
import jax.numpy as jnp
import numpy as np
from jax import lax
from jax.experimental import pallas as pl
from jax.experimental.pallas import tpu as pltpu
from jax.sharding import PartitionSpec as P

ITERS = 5
STRIDES = (1, 4, 16)
GRID = (4, 4, 16)
NSUB = 256
FACES = 6
FD = 256
DOFS = FACES * FD
LOADS = 128
CORNERS = 24
COARSE = 768
NEAR = 256
DOTS = 8
TURN = (0, 2, 4, 1, 3, 5)
EARLY = (0, 1)
PACKED = FD + 2 * CORNERS + 8
PLACES = np.arange(NSUB).reshape(4, 8, 8)
PLANES = PLACES.transpose(1, 0, 2).reshape(8, 32).tolist()
LINES = PLACES.transpose(0, 2, 1).reshape(32, 8).tolist()
PLANE = 32
LINE = 8
ROWS = COARSE // PLANE
f32 = jnp.float32
bf16 = jnp.bfloat16


def route(direction, sign):
    stride, extent = STRIDES[direction], GRID[direction]
    pairs = []
    for i in range(NSUB):
        place = i // stride % extent
        if 0 <= place + sign < extent:
            pairs.append((i, i + sign * stride))
    return pairs


UP = [route(d, 1) for d in range(3)]
DOWN = [route(d, -1) for d in range(3)]


def swap_faces(blocks):
    return [
        lax.ppermute(blocks[f ^ 1], "sub", UP[f // 2] if f % 2 else DOWN[f // 2]) for f in TURN
    ]


def block_of(shape, kind):
    if kind == "smem":
        return pl.BlockSpec(memory_space=pltpu.SMEM)
    if kind == "held":
        return pl.BlockSpec(memory_space=pl.ANY)
    if kind == "rows":
        return pl.BlockSpec((FD, shape[1]), lambda f: (f, 0))
    if kind == "columns":
        return pl.BlockSpec((shape[0], FD), lambda f: (0, f))
    return pl.BlockSpec(shape, lambda f: (0,) * len(shape))


def call(kernel, steps, outs, inputs, scratch=(), flops=0, alias={}):
    inputs = [x if isinstance(x, tuple) else (x, "whole") for x in inputs]
    outs = [x if len(x) == 3 else (*x, "whole") for x in outs]
    size = sum(int(np.prod(s)) * jnp.dtype(t).itemsize for s, t, _ in outs)
    size += sum(x.size * x.dtype.itemsize for x, _ in inputs)
    return pl.pallas_call(
        kernel,
        grid=(steps,),
        out_shape=[jax.ShapeDtypeStruct(s, t) for s, t, _ in outs],
        in_specs=[block_of(x.shape, kind) for x, kind in inputs],
        out_specs=[block_of(s, kind) for s, _, kind in outs],
        scratch_shapes=list(scratch),
        input_output_aliases=alias,
        compiler_params=pltpu.CompilerParams(vmem_limit_bytes=56 * 2**20),
        cost_estimate=pl.CostEstimate(flops=flops, bytes_accessed=size, transcendentals=0),
    )(*[x for x, _ in inputs])


def mm(a, b):
    return lax.dot_general(a, b, (((1,), (0,)), ((), ())), preferred_element_type=f32)


def mm_t(a, b):
    return lax.dot_general(a, b, (((1,), (1,)), ((), ())), preferred_element_type=f32)


def split(values):
    high = values.astype(bf16)
    return high, (values - high.astype(f32)).astype(bf16)


def split3(values):
    high = values.astype(bf16)
    rest = values - high.astype(f32)
    middle = rest.astype(bf16)
    return high, middle, (rest - middle.astype(f32)).astype(bf16)


def face(f):
    return slice(f * FD, (f + 1) * FD)


def order_of(links_ref, f):
    place = lax.broadcasted_iota(jnp.int32, (FD, FD), 0)
    return jnp.where(place == links_ref[f : f + 1, :], 1.0, 0.0).astype(bf16)


def reorder(order, values):
    high, middle, low = split3(values)
    both = mm(order, jnp.concatenate([high, middle], 1))
    return both[:, :LOADS] + both[:, LOADS:] + mm(order, low)


def pack_kernel(jumps, coupling, links, ids, couple, halves, *packs):
    for f in range(FACES):
        part = coupling[:, face(f)]
        jump = jumps[face(f), :]
        if f % 2:
            order = order_of(links, f)
            jump = -reorder(order, jump)
            high, middle, low = split3(part)
            part = -(mm_t(high, order) + mm_t(middle, order) + mm_t(low, order))
        couple[:, face(f)] = part
        high, low = split(part)
        both = jnp.concatenate([high.astype(f32), low.astype(f32)], 0)
        halves[:, face(f)] = both.astype(bf16)
        packs[f][:FD, :] = jump
        packs[f][FD : FD + CORNERS, :] = part[:, :LOADS]
        packs[f][FD + CORNERS : FD + 2 * CORNERS, :] = part[:, LOADS:]
        packs[f][FD + 2 * CORNERS :, :] = ids[...]


def arrange_kernel(schur, links, weights, schur_out, weights_out, half):
    for f in range(FACES):
        if f % 2:
            order = order_of(links, f)
            half[face(f), :] = (-mm(order, schur[face(f), :])).astype(bf16)
            weights_out[face(f), :] = reorder(order, weights[face(f), :])
        else:
            half[face(f), :] = schur[face(f), :]
            weights_out[face(f), :] = weights[face(f), :]
    for f in range(FACES):
        if f % 2:
            order = order_of(links, f)
            schur_out[:, face(f)] = (-mm_t(half[:, face(f)], order)).astype(bf16)
        else:
            schur_out[:, face(f)] = half[:, face(f)]


def lift_kernel(*refs):
    glued, couple = refs[:2]
    packs = [refs[2 + TURN.index(f)] for f in range(FACES)]
    high, low, rows = refs[2 + FACES :]
    step = pl.program_id(0)
    mask = glued[0, step].astype(f32)
    rows[...] = jnp.zeros_like(rows)
    rows[:CORNERS, :] = couple[...] * mask
    for f in range(FACES):

        @pl.when(step == f)
        def _():
            start = CORNERS * (f + 1)
            rows[start : start + CORNERS, :LOADS] = packs[f][FD : FD + CORNERS, :] * mask
            rows[start : start + CORNERS, LOADS:] = (
                packs[f][FD + CORNERS : FD + 2 * CORNERS, :] * mask
            )

    both = split(rows[...].T)
    high[...] = both[0]
    low[...] = both[1]


def open_face(weights, halves, residual, precond, rounded, state, terms):
    now = weights * residual
    precond[...] = now
    high, low = split(now)
    rounded[...] = high
    state[0:1, :] += 0.5 * jnp.sum(now * residual, 0, keepdims=True)
    terms[...] += mm(halves, jnp.concatenate([high, low], 1))


def place_terms(ids, terms, spread):
    total = terms[:, :LOADS] + terms[:, LOADS:]
    total = total[:CORNERS] + total[CORNERS:]
    spread[...] = jnp.zeros_like(spread)
    for j in range(CORNERS):
        spread[pl.ds(ids[0, j], 1), :] = total[j : j + 1]


def begin_kernel(*refs):
    glued, ids, halves, weights = refs[:4]
    sent = refs[4 : 4 + FACES]
    got = [refs[4 + FACES + TURN.index(f)] for f in range(FACES)]
    residual, precond, rounded, spread, state, terms = refs[4 + 2 * FACES :]
    step = pl.program_id(0)

    @pl.when(step == 0)
    def _():
        state[...] = jnp.zeros_like(state)
        terms[...] = jnp.zeros_like(terms)

    for f in range(FACES):

        @pl.when(step == f)
        def _():
            residual[...] = glued[0, f].astype(f32) * (sent[f][:FD, :] + got[f][:FD, :])

    open_face(weights[...], halves[...], residual[...], precond, rounded, state, terms)

    @pl.when(step == FACES - 1)
    def _():
        place_terms(ids, terms, spread)


def local_kernel(schur, rounded, precond, state, *refs):
    faces, local, dots = refs[:FACES], refs[FACES], refs[FACES + 1]
    step = pl.program_id(0)
    now = mm(schur[...], rounded[...])
    local[...] = now
    for f in range(FACES):

        @pl.when(step == f)
        def _():
            faces[f][...] = now

    @pl.when(step == 0)
    def _():
        dots[...] = state[...]

    dots[1:2, :] += jnp.sum(now * precond[...], 0, keepdims=True)


def fold_plane_kernel(parts, dots, out):
    total = jnp.sum(parts[...], 0)
    for i in range(LINE):
        out[i, :ROWS, :] = total
        out[i, ROWS:, :] = dots[...]


def fold_line_kernel(parts, *refs):
    out = refs[-1]
    total = jnp.sum(parts[...], 0)
    for i in range(PLANE):
        out[i] = total


def advance_kernel(first, last, *refs):
    glued, ids, near_ids, whole, inverse_high, inverse_low, lift_high, lift_low = refs[:8]
    local, got, refs = refs[8], [refs[9 + TURN.index(f)] for f in range(FACES)], refs[9 + FACES :]
    weights, precond, residual, history = refs[:4]
    refs = refs[4:]
    if not first:
        multipliers, direction, image = refs[:3]
        refs = refs[3:]
    if last:
        links, multipliers_out, residual_out = refs[:3]
    else:
        halves, multipliers_out, residual_out, direction_out, image_out = refs[:5]
        history_out, precond_out, rounded, spread, state = refs[5:10]
    solved, near, near_both, scalars, partner, terms = refs[-6:]
    face_id = pl.program_id(0)

    @pl.when(face_id == 0)
    def _():
        coarse = whole[:, :ROWS, :].reshape(COARSE, LOADS)
        sums = jnp.sum(whole[:, ROWS:, :], 0)
        coarse_high, coarse_low = split(coarse)
        both = mm(inverse_high[...], jnp.concatenate([coarse_high, coarse_low], 1))
        solution_rows = both[:, :LOADS] + both[:, LOADS:] + mm(inverse_low[...], coarse_high)
        solved[...] = solution_rows
        near[...] = jnp.zeros_like(near)
        for j in range(CORNERS * (FACES + 1)):
            near[pl.ds(j, 1), :] = solved[pl.ds(near_ids[0, j], 1), :]
        near_high, near_low = split(near[...])
        near_both[...] = jnp.concatenate([near_high, near_low], 1)
        energy = sums[0:1]
        curvature = sums[1:2] + jnp.sum(coarse * solution_rows, 0, keepdims=True)
        if not first:
            ratio = energy / history[0:1, :]
            curvature = curvature + ratio * (2.0 * sums[2:3] + ratio * history[1:2, :])
            scalars[1:2, :] = ratio
        scalars[0:1, :] = energy / curvature
        if not last:
            history_out[0:1, :] = energy
            history_out[1:2, :] = curvature
            state[...] = jnp.zeros_like(state)
            terms[...] = jnp.zeros_like(terms)

    for f in range(FACES):

        @pl.when(face_id == f)
        def _():
            partner[...] = got[f][...]

    mask = glued[0, face_id].astype(f32)
    lift = mm(lift_high[...], near_both[...])
    lift = lift[:, :LOADS] + lift[:, LOADS:] + mm(lift_low[...], near_both[:, :LOADS])
    now = mask * (local[...] + partner[...]) + lift
    way = precond[...]
    step = scalars[0:1, :]
    if not first:
        ratio = scalars[1:2, :]
        now = now + ratio * image[...]
        way = way + ratio * direction[...]
    move = step * way
    if not first:
        move = multipliers[...] + move
    rest = residual[...] - step * now
    if last:
        multipliers_out[...] = move
        residual_out[...] = rest

        @pl.when(face_id % 2 == 1)
        def _():
            place = lax.broadcasted_iota(jnp.int32, (FD, FD), 0)
            order = jnp.where(place == links[pl.ds(face_id, 1), :], 1.0, 0.0).T.astype(bf16)
            multipliers_out[...] = reorder(order, move)
            residual_out[...] = reorder(order, rest)

    else:
        multipliers_out[...] = move
        residual_out[...] = rest
        direction_out[...] = way
        image_out[...] = now
        open_face(weights[...], halves[...], rest, precond_out, rounded, state, terms)
        state[2:3, :] += 0.5 * jnp.sum(weights[...] * rest * now, 0, keepdims=True)

        @pl.when(face_id == FACES - 1)
        def _():
            place_terms(ids, terms, spread)


def shards(jumps, schur, coupling, coarse_inverse, scaling, glued, matching, corners):
    links = matching[0]
    field = ((DOFS, LOADS), f32, "rows")
    small = ((DOTS, LOADS), f32)
    open_outs = [field, ((DOFS, LOADS), bf16, "rows"), ((COARSE, LOADS), f32), small]
    terms = pltpu.VMEM((2 * CORNERS, 2 * LOADS), f32)
    masks = (glued, "smem")
    own_ids = (corners, "smem")

    ids_row = jnp.pad(corners.astype(f32), ((0, 7), (0, LOADS - CORNERS)))
    couple, halves, *sent = call(
        pack_kernel,
        1,
        [((CORNERS, DOFS), f32), ((2 * CORNERS, DOFS), bf16)] + [((PACKED, LOADS), f32)] * FACES,
        [jumps[0], coupling[0], links, ids_row],
    )
    halves = (halves, "columns")
    got = swap_faces(sent)
    schur_block, weights = call(
        arrange_kernel,
        1,
        [((DOFS, DOFS), bf16), ((DOFS, LOADS), f32)],
        [schur[0], links, jnp.broadcast_to(scaling[0][:, None], (DOFS, LOADS))],
        scratch=[pltpu.VMEM((DOFS, DOFS), bf16)],
        flops=4 * DOFS * DOFS * FD,
    )
    weights = (weights, "rows")
    residual, precond, rounded, spread, state = call(
        begin_kernel,
        FACES,
        [field] + open_outs,
        [masks, own_ids, halves, weights, *sent, *got],
        scratch=[terms],
    )
    lift_high, lift_low = call(
        lift_kernel,
        FACES,
        [((DOFS, NEAR), bf16, "rows")] * 2,
        [masks, (couple, "columns"), *got],
        scratch=[pltpu.VMEM((NEAR, FD), f32)],
    )
    near_ids = jnp.concatenate(
        [corners]
        + [
            got[TURN.index(f)][FD + 2 * CORNERS :][:1, :CORNERS].astype(jnp.int32)
            for f in range(FACES)
        ],
        1,
    )
    kept = lax.reduce_precision(coarse_inverse, 8, 7)
    inverse_high, inverse_low = kept.astype(bf16), (coarse_inverse - kept).astype(bf16)

    multipliers = direction = image = history = None
    for iteration in range(ITERS):
        first, last = iteration == 0, iteration + 1 == ITERS
        parts = lax.all_to_all(
            spread.reshape(PLANE, ROWS, LOADS), "sub", 0, 0, axis_index_groups=PLANES
        )
        *faces, local, dots = call(
            local_kernel,
            FACES,
            [((FD, LOADS), f32)] * FACES + [field, small],
            [(schur_block, "rows"), rounded, (precond, "rows"), state],
            flops=2 * DOFS * DOFS * LOADS,
        )
        received = swap_faces(faces)
        early = [(received[TURN.index(f)], "held") for f in EARLY]
        (lines,) = call(fold_plane_kernel, 1, [((LINE, ROWS + DOTS, LOADS), f32)], [parts, dots])
        lines = lax.all_to_all(lines, "sub", 0, 0, axis_index_groups=LINES)
        (whole,) = call(fold_line_kernel, 1, [((PLANE, ROWS + DOTS, LOADS), f32)], [lines, *early])
        whole = lax.all_to_all(whole, "sub", 0, 0, axis_index_groups=PLANES)
        inputs = [masks, own_ids, (near_ids, "smem"), whole, inverse_high, inverse_low]
        inputs += [(lift_high, "rows"), (lift_low, "rows"), (local, "rows"), *received]
        inputs += [weights, (precond, "rows"), (residual, "rows"), state if first else history]
        if not first:
            inputs += [(multipliers, "rows"), (direction, "rows"), (image, "rows")]
        inputs += [links if last else halves]
        outs = [field, field]
        if not last:
            outs += [field, field, small] + open_outs
        results = call(
            functools.partial(advance_kernel, first, last),
            FACES,
            outs,
            inputs,
            scratch=[
                pltpu.VMEM((COARSE, LOADS), f32),
                pltpu.VMEM((NEAR, LOADS), f32),
                pltpu.VMEM((NEAR, 2 * LOADS), bf16),
                pltpu.VMEM((8, LOADS), f32),
                pltpu.VMEM((FD, LOADS), f32),
                terms,
            ],
        )
        multipliers, residual = results[:2]
        if not last:
            direction, image, history, precond, rounded, spread, state = results[2:]
    return (multipliers[None], residual[None])


def solution(mesh):
    return jax.shard_map(
        shards,
        mesh=mesh,
        in_specs=(
            P("sub", None, None),
            P("sub", None, None),
            P("sub", None, None),
            P(),
            P("sub", None),
            P("sub", None),
            P("sub", None, None),
            P("sub", None),
        ),
        out_specs=(P("sub", None, None), P("sub", None, None)),
        check_vma=False,
    )
```
